128 devices in a mesh: rep: 8 (over y, z_hi), fsdp: 16 (over x, z_lo, core).
Axes of the slice: x: 4, y: 4, z: 4 (z_hi: 2, z_lo: 2; z = z_hi * 2 + z_lo), core: 2. Of those that a mesh axis runs over, the one named last changes fastest.
Arguments:
- tokens: bfloat16 [65536, 8192], P(('rep', 'fsdp')), may hold values from -6 to 6
- gain: float32 [8192], replicated, may hold values from 0.5 to 1.5
- value_weight: bfloat16 [8, 8192, 1024], P('rep', 'fsdp'), may hold values from -0.0625 to 0.0625
- cotangent: bfloat16 [65536, 1024], P(('rep', 'fsdp')), may hold values from -3 to 3
- codes: bfloat16 [8, 8192, 1024], P('rep', 'fsdp'), may hold values from -4 to 4
- scales: bfloat16 [8, 8192, 8], P('rep', 'fsdp'), may hold values from 0.049804688 to 0.5
- local_frag: bfloat16 [8, 8192, 1024], P('rep', 'fsdp'), may hold values from -6 to 6
- momentum: float32 [8192, 1024], P('fsdp', 'rep'), may hold values from -3 to 3
- global_frag: float32 [8192, 1024], P('fsdp', 'rep'), may hold values from -6 to 6
Outputs:
- values_out: bfloat16 [65536, 1024], P(('rep', 'fsdp'))
- token_gradient: bfloat16 [65536, 8192], P(('rep', 'fsdp'))
- weight_grad: bfloat16 [8, 8192, 1024], P('rep', 'fsdp')
- merged_frag: bfloat16 [8, 8192, 1024], P('rep', 'fsdp')
- new_momentum: float32 [8192, 1024], P('fsdp', 'rep')
- new_global: float32 [8192, 1024], P('fsdp', 'rep')
The draws below stay inside these ranges and needn't reach their ends.
All inputs are finite; a program needn't handle non-finite values.
Results may differ from the reference program's by a relative error of at most 0.022.
Values may be sent and summed in bfloat16 or wider, within the bound.
No kernel may reach another device: no remote copies, remote signals or barrier semaphores. Data moves between devices by JAX's collectives and lax.ppermute only.
A program may use at most 192 MiB of HBM per device.

```python
import math
import jax
import jax.numpy as jnp
from jax import lax

D = 8192
KV = 1024
TOK_DEV = 512
SCALE_BLOCK = 128
FRAG_ROWS = 8192
TOKENS = 65536
N_REP = 8
N_FSDP = 16


def levels(rng, dims, pieces, smallest, high):
    loudness, own = 1.0, jax.random.fold_in(rng, 6)
    for position, blocks in pieces:
        steps = jnp.exp(jax.random.uniform(jax.random.fold_in(own, position), (blocks,), jnp.float32, smallest / len(pieces), high / len(pieces)))
        loudness = loudness * jnp.repeat(steps, dims[position] // blocks).reshape([-1 if axis == position else 1 for axis in range(len(dims))])
    return loudness


def bell_draw(own_key, shape, scale, reach, split=(), kind=jnp.bfloat16):
    factor_of = levels(own_key, shape, split, -0.22, 0.18) if split else 1.0
    array = jax.random.normal(own_key, shape, jnp.float32) * scale * factor_of
    return jnp.minimum(jnp.maximum(array, -reach), reach).astype(kind)


def setup_inputs(seed: int = 0) -> dict:
    key_list = jax.random.split(jax.random.key(seed), 10)
    tokens = bell_draw(key_list[0], (TOKENS, D), 1.0, 6.0, ((0, 128),))
    gain = jnp.clip(1.0 + 0.1 * jax.random.normal(key_list[1], (D,), jnp.float32), 0.5, 1.5)
    value_weight = bell_draw(key_list[2], (N_REP, D, KV), D ** -0.5, 0.0625, ((0, 8), (1, 16)))
    cotangent = bell_draw(key_list[3], (TOKENS, KV), 0.5, 3.0, ((0, 128),))
    codes = bell_draw(key_list[4], (N_REP, FRAG_ROWS, KV), 1.0, 4.0, ((0, 8), (1, 16)))
    scales = jnp.clip(jnp.exp(math.log(0.5) - 2.306499 * jax.random.uniform(key_list[5], (N_REP, FRAG_ROWS, KV // SCALE_BLOCK), jnp.float32) ** levels(key_list[5], (N_REP, FRAG_ROWS, KV // SCALE_BLOCK), ((0, 8), (1, 16)), -0.2, 0.2)), 0.049804688, 0.5).astype(jnp.bfloat16)
    local_frag = bell_draw(key_list[6], (N_REP, FRAG_ROWS, KV), 1.0, 6.0, ((0, 8), (1, 16)))
    momentum = bell_draw(key_list[7], (FRAG_ROWS, KV), 0.5, 3.0, ((0, 16), (1, 8)), jnp.float32)
    global_frag = bell_draw(key_list[8], (FRAG_ROWS, KV), 1.0, 6.0, ((0, 16), (1, 8)), jnp.float32)
    return dict(tokens=tokens, gain=gain, value_weight=value_weight, cotangent=cotangent, codes=codes, scales=scales, local_frag=local_frag, momentum=momentum, global_frag=global_frag)


def reference(tokens, gain, value_weight, cotangent, codes, scales, local_frag, momentum, global_frag):
    token_input = tokens.astype(jnp.float32)
    inverse_root_mean = 1.0 / jnp.sqrt(lax.optimization_barrier(jnp.mean(token_input * token_input, axis=-1, keepdims=True)) + 1e-05)
    centered_tokens = token_input * inverse_root_mean
    normalized_input = (centered_tokens * gain).astype(jnp.bfloat16)
    per_rep = N_FSDP * TOK_DEV
    normed_r = normalized_input.reshape(N_REP, per_rep, D)
    cot_r = cotangent.reshape(N_REP, per_rep, KV)

    def one_replica(items):
        xs, cs, weight = items
        outs = jnp.dot(xs, weight, preferred_element_type=jnp.float32)
        back = jnp.dot(cs, weight.T, preferred_element_type=jnp.float32)

        def add_block(total, block):
            xb, cb = block
            part = jnp.dot(xb.T, cb, preferred_element_type=jnp.float32) / N_FSDP
            return (total + part.astype(jnp.bfloat16).astype(jnp.float32), 0)
        total, _ = lax.scan(add_block, jnp.zeros((D, KV), jnp.float32), (xs.reshape(N_FSDP, TOK_DEV, D), cs.reshape(N_FSDP, TOK_DEV, KV)))
        return (outs, back, total)
    outs, back, grads = lax.map(one_replica, (normed_r, cot_r, value_weight))
    values_out = outs.reshape(TOKENS, KV).astype(jnp.bfloat16)
    norm_gain = back.reshape(TOKENS, D) * gain
    token_gradient = (inverse_root_mean * (norm_gain - centered_tokens * lax.optimization_barrier(jnp.mean(norm_gain * centered_tokens, axis=-1, keepdims=True)))).astype(jnp.bfloat16)
    weight_grad = grads.astype(jnp.bfloat16)
    block_groups = KV // SCALE_BLOCK
    delta = (codes.astype(jnp.float32).reshape(N_REP, FRAG_ROWS, block_groups, SCALE_BLOCK) * scales.astype(jnp.float32)[..., None]).reshape(N_REP, FRAG_ROWS, KV)
    average = lax.optimization_barrier(jnp.sum(delta, axis=0)) / N_REP
    new_momentum = 0.9 * momentum + average
    new_global = global_frag - 0.7 * (average + 0.9 * new_momentum)
    merged_frag = (0.5 * local_frag.astype(jnp.float32) + 0.5 * new_global[None]).astype(jnp.bfloat16)
    return (values_out, token_gradient, weight_grad, merged_frag, new_momentum, new_global)
```

```python
import jax
import jax.numpy as jnp
from jax import lax
from jax.experimental import pallas as pl
from jax.experimental.pallas import tpu as pltpu
from jax.sharding import PartitionSpec as P

F32 = jnp.float32
BF16 = jnp.bfloat16
NX, NZ, NC, NY, NH = 4, 2, 2, 4, 2
NEAR = ((0, 0), (1, 0), (3, 0), (0, 1))
FAR = ((2, 0), (1, 1), (3, 1), (2, 1))
VMEM = 40 * 2**20


def fsdp_index(x, z, c):
    return ((x % NX) * NZ + z % NZ) * NC + c % NC


def move(value, dx=0, dz=0, dc=0):
    pairs = [
        (fsdp_index(x, z, c), fsdp_index(x + dx, z + dz, c + dc))
        for x in range(NX)
        for z in range(NZ)
        for c in range(NC)
    ]
    return lax.ppermute(value, "fsdp", pairs)


def move_rep(value, dy=0, dh=0):
    pairs = [
        (y * NH + h, ((y + dy) % NY) * NH + (h + dh) % NH) for y in range(NY) for h in range(NH)
    ]
    return lax.ppermute(value, "rep", pairs)


def shard_order(places, dc):
    me = lax.axis_index("fsdp")
    x, z, c = me // (NZ * NC), (me // NC) % NZ, me % NC
    return jnp.stack([fsdp_index(x + dx, z + dz, c + dc) for dx, dz in places]).astype(jnp.int32)


def params():
    return pltpu.CompilerParams(
        vmem_limit_bytes=VMEM, dimension_semantics=("arbitrary",)
    )


def weight_term(tokens, gain, scaled_cot, order, other, groups):
    rows, width = tokens.shape
    outs = scaled_cot.shape[1]
    count = order.shape[0]
    depth = width // (NX * NZ * NC)

    def body(order_ref, tok_ref, gain_ref, cot_ref, *rest):
        out_ref = rest[-1]
        left = (tok_ref[...].astype(F32) * gain_ref[...]).astype(BF16)
        term = lax.dot_general(
            left, cot_ref[...], (((0,), (0,)), ((), ())), preferred_element_type=F32
        ) * (1.0 / groups)
        if len(rest) > 1:
            term = term + rest[0][0].astype(F32)
        out_ref[0] = term.astype(BF16)

    block = pl.BlockSpec((1, depth, outs), lambda k, o: (k, 0, 0))
    in_specs = [
        pl.BlockSpec((rows, depth), lambda k, o: (0, o[k])),
        pl.BlockSpec((1, depth), lambda k, o: (0, o[k])),
        pl.BlockSpec((rows, outs), lambda k, o: (0, 0)),
    ]
    args = [order, tokens, gain, scaled_cot]
    if other is not None:
        in_specs.append(block)
        args.append(other)
    return pl.pallas_call(
        body,
        out_shape=jax.ShapeDtypeStruct((count, depth, outs), BF16),
        grid_spec=pltpu.PrefetchScalarGridSpec(
            num_scalar_prefetch=1, grid=(count,), in_specs=in_specs, out_specs=block
        ),
        compiler_params=params(),
        cost_estimate=pl.CostEstimate(
            flops=2 * rows * depth * count * outs,
            bytes_accessed=count * depth * (rows + 2 * outs) * 2,
            transcendentals=0,
        ),
    )(*args)


def forward(tokens, gain, order, weights, total):
    rows, width = tokens.shape
    count, depth, outs = weights.shape

    def body(order_ref, tok_ref, gain_ref, w_ref, *rest):
        out_ref = rest[-1]
        left = (tok_ref[...].astype(F32) * gain_ref[...]).astype(BF16)
        term = jnp.dot(left, w_ref[0], preferred_element_type=F32)

        @pl.when(pl.program_id(0) == 0)
        def _():
            out_ref[...] = term + rest[0][...] if len(rest) > 1 else term

        @pl.when(pl.program_id(0) > 0)
        def _():
            out_ref[...] += term

    whole = pl.BlockSpec((rows, outs), lambda k, o: (0, 0))
    in_specs = [
        pl.BlockSpec((rows, depth), lambda k, o: (0, o[k])),
        pl.BlockSpec((1, depth), lambda k, o: (0, o[k])),
        pl.BlockSpec((1, depth, outs), lambda k, o: (k, 0, 0)),
    ]
    args = [order, tokens, gain, weights]
    if total is not None:
        in_specs.append(whole)
        args.append(total)
    return pl.pallas_call(
        body,
        out_shape=jax.ShapeDtypeStruct((rows, outs), F32),
        grid_spec=pltpu.PrefetchScalarGridSpec(
            num_scalar_prefetch=1, grid=(count,), in_specs=in_specs, out_specs=whole
        ),
        compiler_params=params(),
        cost_estimate=pl.CostEstimate(
            flops=2 * rows * depth * count * outs,
            bytes_accessed=count * depth * (rows + outs) * 2,
            transcendentals=0,
        ),
    )(*args)


def backward(tokens, gain, cotangent, rinv, mean, order, weights):
    rows, width = tokens.shape
    per, depth, outs = weights[0].shape
    sets = len(weights)

    def body(order_ref, tok_ref, gain_ref, cot_ref, rinv_ref, mean_ref, *rest):
        out_ref = rest[-1]
        step = pl.program_id(0)
        scale = rinv_ref[...]

        def one(w_ref):
            back = lax.dot_general(
                cot_ref[...], w_ref[0], (((1,), (1,)), ((), ())), preferred_element_type=F32
            )
            hat = tok_ref[...].astype(F32) * scale
            out_ref[...] = (scale * (back * gain_ref[...] - hat * mean_ref[...])).astype(BF16)

        for j in range(sets):
            pl.when(step // per == j)(lambda j=j: one(rest[j]))

    def weight_spec(j):
        return pl.BlockSpec(
            (1, depth, outs), lambda k, o: (jnp.clip(k - j * per, 0, per - 1), 0, 0)
        )

    column = pl.BlockSpec((rows, 1), lambda k, o: (0, 0))
    block = pl.BlockSpec((rows, depth), lambda k, o: (0, o[k]))
    return pl.pallas_call(
        body,
        out_shape=jax.ShapeDtypeStruct((rows, width), BF16),
        grid_spec=pltpu.PrefetchScalarGridSpec(
            num_scalar_prefetch=1,
            grid=(per * sets,),
            in_specs=[
                block,
                pl.BlockSpec((1, depth), lambda k, o: (0, o[k])),
                pl.BlockSpec((rows, outs), lambda k, o: (0, 0)),
                column,
                column,
            ]
            + [weight_spec(j) for j in range(sets)],
            out_specs=block,
        ),
        compiler_params=params(),
        cost_estimate=pl.CostEstimate(
            flops=2 * rows * width * outs,
            bytes_accessed=width * (2 * rows + outs) * 2,
            transcendentals=0,
        ),
    )(order, tokens, gain, cotangent, rinv, mean, *weights)


def gather_weight(own):
    depth = own.shape[0]
    half = depth // 2
    a, b = (depth // 3 + 15) // 16 * 16, depth - (depth // 3 + 15) // 16 * 16
    xm = move(own, dx=1)
    xp = move(own, dx=-1)
    zz = move(own, dz=1)
    near = jnp.stack([own, xp, xm, zz])
    near_other = move(near, dc=1)
    r1 = move(jnp.concatenate([zz[:half], xm[:half]]), dx=1)
    r2 = move(jnp.concatenate([zz[:half], xp[half:]]), dx=-1)
    r3 = move(jnp.concatenate([xp[half:], xm[half:]]), dz=1)
    x2 = jnp.concatenate([r1[half:], r2[half:]])
    zxp = jnp.concatenate([r2[:half], r3[:half]])
    zxm = jnp.concatenate([r1[:half], r3[half:]])
    r4 = move(zxm[:a], dx=1)
    r5 = move(zxp[b:], dx=-1)
    r6 = move(x2[a:b], dz=1)
    zx2 = jnp.concatenate([r4, r6, r5])
    far = jnp.stack([x2, zxp, zxm, zx2])
    far_other = move(far, dc=1)
    return near, near_other, far, far_other


def add(*terms):
    total = terms[0].astype(F32)
    for term in terms[1:]:
        total = total + term.astype(F32)
    return total.astype(BF16)


def scatter_grad(far, near):
    x2, zxp, zxm, zx2 = (far[i] for i in range(4))
    own, xp, xm, zz = (near[i] for i in range(4))
    depth = own.shape[0]
    half = depth // 2
    a, b = (depth // 3 + 15) // 16 * 16, depth - (depth // 3 + 15) // 16 * 16
    q4 = move(zx2[:a], dx=-1)
    q5 = move(zx2[b:], dx=1)
    q6 = move(zx2[a:b], dz=1)
    q1 = move(
        jnp.concatenate(
            [add(zxm[:a], q4), zxm[a:half], x2[:a], add(x2[a:half], q6[: half - a])]
        ),
        dx=-1,
    )
    q2 = move(
        jnp.concatenate([zxp[:half], add(x2[half:b], q6[half - a :]), x2[b:]]), dx=1
    )
    q3 = move(jnp.concatenate([zxp[half:b], add(zxp[b:], q5), zxm[half:]]), dz=1)
    sxp = move(jnp.concatenate([xp[:half], add(xp[half:], q2[half:], q3[:half])]), dx=1)
    sxm = move(
        jnp.concatenate([add(xm[:half], q1[half:]), add(xm[half:], q3[half:])]), dx=-1
    )
    szz = move(jnp.concatenate([add(zz[:half], q1[:half], q2[:half]), zz[half:]]), dz=1)
    return add(own, sxp, sxm, szz)


def outer_step(codes, scales, local_frag, momentum, global_frag):
    rows, width = codes.shape
    blocks = scales.shape[1]
    delta = (
        (
            codes.astype(F32).reshape(rows, blocks, width // blocks)
            * scales.astype(F32)[..., None]
        )
        .reshape(rows, width)
        .astype(BF16)
    )
    me = lax.axis_index("rep")
    y, h = me // NH, me % NH
    wide = width // NY
    piece = wide // NH
    def columns(value, k):
        return lax.dynamic_slice_in_dim(value, ((y + k) % NY) * wide, wide, axis=1)
    total = columns(delta, 0).astype(F32)
    for got in [move_rep(columns(delta, k), dy=k) for k in range(1, NY)]:
        total = total + got.astype(F32)
    mine = lax.dynamic_slice_in_dim(total, h * piece, piece, axis=1)
    theirs = lax.dynamic_slice_in_dim(total, (1 - h) * piece, piece, axis=1)
    average = (mine + move_rep(theirs.astype(BF16), dh=1).astype(F32)) / (NY * NH)
    new_momentum = 0.9 * momentum + average
    new_global = global_frag - 0.7 * (average + 0.9 * new_momentum)
    sent = new_global.astype(BF16)
    got = move_rep(sent, dh=1)
    pair = jnp.where(
        h == 0, jnp.concatenate([sent, got], axis=1), jnp.concatenate([got, sent], axis=1)
    )
    full = jnp.zeros((rows, width), BF16)
    for k in range(NY):
        part = pair if k == 0 else move_rep(pair, dy=-k)
        full = lax.dynamic_update_slice_in_dim(full, part, ((y + k) % NY) * wide, axis=1)
    merged = (0.5 * local_frag.astype(F32) + 0.5 * full.astype(F32)).astype(BF16)
    return merged, new_momentum, new_global


def per_device(
    tokens, gain, value_weight, cotangent, codes, scales, local_frag, momentum, global_frag
):
    groups = NX * NZ * NC
    width = tokens.shape[1]
    gain_row = gain[None]
    near, near_other, far, far_other = gather_weight(value_weight[0])
    merged, new_momentum, new_global = outer_step(
        codes[0], scales[0], local_frag[0], momentum, global_frag
    )
    token_input = tokens.astype(F32)
    rinv = 1.0 / jnp.sqrt(jnp.mean(token_input * token_input, axis=-1, keepdims=True) + 1e-05)
    scaled_cot = (cotangent.astype(F32) * rinv).astype(BF16)
    own_order = [shard_order(FAR, 0), shard_order(NEAR, 0)]
    other_order = [shard_order(FAR, 1), shard_order(NEAR, 1)]
    terms = []
    for mine, theirs in zip(own_order, other_order):
        sent = weight_term(tokens, gain_row, scaled_cot, theirs, None, groups)
        terms.append(
            weight_term(tokens, gain_row, scaled_cot, mine, move(sent, dc=1), groups)
        )
    weight_grad = scatter_grad(*terms)

    total = None
    for weights, order in (
        (near, own_order[1]),
        (near_other, other_order[1]),
        (far, own_order[0]),
        (far_other, other_order[0]),
    ):
        total = forward(tokens, gain_row, order, weights, total)
    outs = total * rinv
    mean = jnp.sum(outs * cotangent.astype(F32), axis=-1, keepdims=True) / width
    token_gradient = backward(
        tokens,
        gain_row,
        cotangent,
        rinv,
        mean,
        jnp.concatenate([own_order[1], other_order[1], own_order[0], other_order[0]]),
        (near, near_other, far, far_other),
    )
    return (
        outs.astype(BF16),
        token_gradient,
        weight_grad[None],
        merged[None],
        new_momentum,
        new_global,
    )


def solution(mesh):
    return jax.shard_map(
        per_device,
        mesh=mesh,
        in_specs=(
            P(("rep", "fsdp"), None),
            P(),
            P("rep", "fsdp", None),
            P(("rep", "fsdp"), None),
            P("rep", "fsdp", None),
            P("rep", "fsdp", None),
            P("rep", "fsdp", None),
            P("fsdp", "rep"),
            P("fsdp", "rep"),
        ),
        out_specs=(
            P(("rep", "fsdp"), None),
            P(("rep", "fsdp"), None),
            P("rep", "fsdp", None),
            P("rep", "fsdp", None),
            P("fsdp", "rep"),
            P("fsdp", "rep"),
        ),
        check_vma=False,
    )
```

```python
import jax
import jax.numpy as jnp
from jax import lax
from jax.experimental import pallas as pl
from jax.experimental.pallas import tpu as pltpu
from jax.sharding import PartitionSpec as P

F32 = jnp.float32
BF16 = jnp.bfloat16
NX, NZ, NC, NY, NH = 4, 2, 2, 4, 2
OWN, XP, XM, ZZ = (0, 0), (1, 0), (3, 0), (0, 1)
X2, ZXP, ZXM, ZX2 = (2, 0), (1, 1), (3, 1), (2, 1)
NEAR = (OWN, XP, XM, ZZ)
FAR = (X2, ZXP, ZXM, ZX2)
VMEM = 62 * 2**20


def fsdp_index(x, z, c):
    return ((x % NX) * NZ + z % NZ) * NC + c % NC


def move(value, dx=0, dz=0, dc=0):
    pairs = [
        (fsdp_index(x, z, c), fsdp_index(x + dx, z + dz, c + dc))
        for x in range(NX)
        for z in range(NZ)
        for c in range(NC)
    ]
    return lax.ppermute(value, "fsdp", pairs)


def swap_rep(value, y_bit=0, h_bit=0):
    pairs = [(y * NH + h, (y ^ y_bit) * NH + (h ^ h_bit)) for y in range(NY) for h in range(NH)]
    return lax.ppermute(value, "rep", pairs)


def halves(places):
    return [(place, part) for place in places for part in (0, 1)]


def order_table(lists):
    me = lax.axis_index("fsdp")
    x, z, c = me // (NZ * NC), (me // NC) % NZ, me % NC
    table = []
    for dc, items in lists:
        for item in items:
            (dx, dz), part = item if isinstance(item[0], tuple) else (item, None)
            index = fsdp_index(x + dx, z + dz, c + dc)
            table.append(index if part is None else index * 2 + part)
    return jnp.stack(table).astype(jnp.int32)


def params():
    return pltpu.CompilerParams(vmem_limit_bytes=VMEM)


SPACE = pl.BlockSpec(memory_space=pltpu.HBM)
LOCAL = pl.BlockSpec(memory_space=pltpu.VMEM)
SCALARS = pl.BlockSpec(memory_space=pltpu.SMEM)
COST = pl.CostEstimate(flops=1, bytes_accessed=1, transcendentals=0)


def statistics(tokens, cotangent):
    rows, width = tokens.shape
    outs = cotangent.shape[1]
    step = rows // 8

    def body(tok_ref, cot_ref, rinv_ref, scaled_ref):
        lanes = 512
        total = jnp.zeros((step, lanes), F32)
        for first in range(0, width, lanes):
            value = tok_ref[:, first : first + lanes].astype(F32)
            total = total + value * value
        mean = jnp.sum(total, axis=-1, keepdims=True) / width
        rinv = 1.0 / jnp.sqrt(mean + 1e-05)
        rinv_ref[...] = rinv
        scaled_ref[...] = (cot_ref[...].astype(F32) * rinv).astype(BF16)

    def block(columns):
        return pl.BlockSpec((step, columns), lambda k: (k, 0))

    return pl.pallas_call(
        body,
        out_shape=(
            jax.ShapeDtypeStruct((rows, 1), F32),
            jax.ShapeDtypeStruct((rows, outs), BF16),
        ),
        grid=(8,),
        in_specs=[block(width), block(outs)],
        out_specs=(block(1), block(outs)),
        compiler_params=params(),
        cost_estimate=COST,
    )(tokens, cotangent)


def unit_columns(order_ref, k, unit):
    return pl.ds(pl.multiple_of(order_ref[k] * unit, unit), unit)


def token_copies(order_ref, base, tok_ref, buf, sem, step, unit, per):
    slot = step % 2
    return [
        pltpu.make_async_copy(
            tok_ref.at[:, unit_columns(order_ref, base + step * per + u, unit)],
            buf.at[slot, :, pl.ds(u * unit, unit)],
            sem.at[slot, u],
        )
        for u in range(per)
    ]


def unit_gain(order_ref, base, gain_ref, step, unit, per):
    return jnp.concatenate(
        [gain_ref[:, unit_columns(order_ref, base + step * per + u, unit)] for u in range(per)],
        axis=1,
    )


def weight_terms(tokens, gain, scaled_cot, order, groups, other=None, first=0):
    rows, width = tokens.shape
    outs = scaled_cot.shape[1]
    unit = width // (NX * NZ * NC * 2)
    order, base, count = order
    depth = 2 * unit
    steps = count // 2

    def body(order_ref, tok_ref, gain_ref, cot_ref, *rest):
        if other is None:
            out_ref, tok_buf, out_buf, tok_sem, out_sem = rest
            targets = [out_ref.at[k] for k in range(count)]
        else:
            other_ref, targets = rest[0], rest[1 : 1 + count]
            tok_buf, out_buf, tok_sem, out_sem, other_buf, other_sem = rest[1 + count :]

        def loads(step):
            copies = token_copies(order_ref, base, tok_ref, tok_buf, tok_sem, step, unit, 4)
            if other is not None:
                copies += [
                    pltpu.make_async_copy(
                        other_ref.at[first + 2 * step + j],
                        other_buf.at[step % 2, j],
                        other_sem.at[step % 2, j],
                    )
                    for j in range(2)
                ]
            return copies

        def stores(step):
            return [
                pltpu.make_async_copy(
                    out_buf.at[step % 2, j], targets[2 * step + j], out_sem.at[step % 2, j]
                )
                for j in range(2)
            ]

        for copy in loads(0):
            copy.start()
        for step in range(steps):
            slot = step % 2
            if step + 1 < steps:
                for copy in loads(step + 1):
                    copy.start()
            for copy in loads(step):
                copy.wait()
            gains = unit_gain(order_ref, base, gain_ref, step, unit, 4)
            left = (tok_buf[slot].astype(F32) * gains).astype(BF16)
            term = lax.dot_general(
                left, cot_ref[...], (((0,), (0,)), ((), ())), preferred_element_type=F32
            ) * (1.0 / groups)
            term = term.reshape(2, depth, outs)
            if other is not None:
                term = term + other_buf[slot].astype(F32)
            if step >= 2:
                for copy in stores(step - 2):
                    copy.wait()
            out_buf[slot] = term.astype(BF16)
            for copy in stores(step):
                copy.start()
        for step in range(max(steps - 2, 0), steps):
            for copy in stores(step):
                copy.wait()

    scratch = [
        pltpu.VMEM((2, rows, 2 * depth), BF16),
        pltpu.VMEM((2, 2, depth, outs), BF16),
        pltpu.SemaphoreType.DMA((2, 4)),
        pltpu.SemaphoreType.DMA((2, 2)),
    ]
    in_specs, args = [SCALARS, SPACE, LOCAL, LOCAL], [order, tokens, gain, scaled_cot]
    if other is None:
        out_shape, out_specs = jax.ShapeDtypeStruct((count, depth, outs), BF16), SPACE
    else:
        out_shape = (jax.ShapeDtypeStruct((depth, outs), BF16),) * count
        out_specs = (SPACE,) * count
        in_specs.append(SPACE)
        args.append(other)
        scratch += [pltpu.VMEM((2, 2, depth, outs), BF16), pltpu.SemaphoreType.DMA((2, 2))]
    return pl.pallas_call(
        body,
        out_shape=out_shape,
        in_specs=in_specs,
        out_specs=out_specs,
        scratch_shapes=scratch,
        compiler_params=params(),
        cost_estimate=COST,
    )(*args)


def unique(sources):
    arrays, places = [], []
    for array, where in sources:
        position = next((i for i, known in enumerate(arrays) if known is array), len(arrays))
        if position == len(arrays):
            arrays.append(array)
        places.append((position, where))
    return arrays, places


def weight_copies(refs, places, buf, sem, step):
    copies = []
    for j in range(2):
        position, where = places[2 * step + j]
        source = refs[position] if where is None else refs[position].at[where]
        copies.append(pltpu.make_async_copy(source, buf.at[step % 2, j], sem.at[step % 2, j]))
    return copies


def forward(tokens, gain, order, sources, total, last=None):
    rows, width = tokens.shape
    arrays, places = unique(sources)
    depth, outs = arrays[0].shape[-2:]
    steps, ins = len(places) // 2, len(arrays)
    order, base = order
    rest_in = (0 if total is None else 1) + (0 if last is None else 2)

    def body(order_ref, tok_ref, gain_ref, *rest):
        extra = rest[ins : ins + rest_in]
        results = rest[ins + rest_in : -4]
        tok_buf, w_buf, tok_sem, w_sem = rest[-4:]

        def loads(step):
            return token_copies(
                order_ref, base, tok_ref, tok_buf, tok_sem, step, depth, 2
            ) + weight_copies(rest[:ins], places, w_buf, w_sem, step)

        for copy in loads(0):
            copy.start()
        acc = None if total is None else extra[0][...]
        for step in range(steps):
            if step + 1 < steps:
                for copy in loads(step + 1):
                    copy.start()
            for copy in loads(step):
                copy.wait()
            gains = unit_gain(order_ref, base, gain_ref, step, depth, 2)
            left = (tok_buf[step % 2].astype(F32) * gains).astype(BF16)
            term = jnp.dot(
                left, w_buf[step % 2].reshape(2 * depth, outs), preferred_element_type=F32
            )
            acc = term if acc is None else acc + term
        if last is None:
            results[0][...] = acc
        else:
            rinv = extra[-2][...]
            results[0][...] = (acc * rinv).astype(BF16)
            dots = jnp.sum(acc * extra[-1][...].astype(F32), axis=-1, keepdims=True)
            results[1][...] = dots * rinv * rinv * (1.0 / width)

    if last is None:
        out_shape, out_specs = jax.ShapeDtypeStruct((rows, outs), F32), LOCAL
    else:
        out_shape = (
            jax.ShapeDtypeStruct((rows, outs), BF16),
            jax.ShapeDtypeStruct((rows, 1), F32),
        )
        out_specs = (LOCAL, LOCAL)
    return pl.pallas_call(
        body,
        out_shape=out_shape,
        in_specs=[SCALARS, SPACE, LOCAL] + [SPACE] * ins + [LOCAL] * rest_in,
        out_specs=out_specs,
        scratch_shapes=[
            pltpu.VMEM((2, rows, 2 * depth), BF16),
            pltpu.VMEM((2, 2, depth, outs), BF16),
            pltpu.SemaphoreType.DMA((2, 2)),
            pltpu.SemaphoreType.DMA((2, 2)),
        ],
        compiler_params=params(),
        cost_estimate=COST,
    )(order, tokens, gain, *arrays, *(() if total is None else (total,)), *(last or ()))


def backward(tokens, gain, scaled_cot, less, order, sources, result):
    rows, width = tokens.shape
    arrays, places = unique(sources)
    depth, outs = arrays[0].shape[-2:]
    steps = len(places) // 2
    order, base = order
    aliased = result is not None

    def body(order_ref, tok_ref, gain_ref, cot_ref, less_ref, *rest):
        refs = rest[: len(arrays)]
        out_ref, tok_buf, w_buf, out_buf, tok_sem, w_sem, out_sem = rest[-7:]

        def loads(step):
            return token_copies(
                order_ref, base, tok_ref, tok_buf, tok_sem, step, depth, 2
            ) + weight_copies(refs, places, w_buf, w_sem, step)

        def stores(step):
            return [
                pltpu.make_async_copy(
                    out_buf.at[step % 2, :, pl.ds(u * depth, depth)],
                    out_ref.at[:, unit_columns(order_ref, base + step * 2 + u, depth)],
                    out_sem.at[step % 2, u],
                )
                for u in range(2)
            ]

        for copy in loads(0):
            copy.start()
        for step in range(steps):
            slot = step % 2
            if step + 1 < steps:
                for copy in loads(step + 1):
                    copy.start()
            for copy in loads(step):
                copy.wait()
            gains = unit_gain(order_ref, base, gain_ref, step, depth, 2)
            back = lax.dot_general(
                cot_ref[...],
                w_buf[slot].reshape(2 * depth, outs),
                (((1,), (1,)), ((), ())),
                preferred_element_type=F32,
            )
            if step >= 2:
                for copy in stores(step - 2):
                    copy.wait()
            out_buf[slot] = (back * gains - tok_buf[slot].astype(F32) * less_ref[...]).astype(
                BF16
            )
            for copy in stores(step):
                copy.start()
        for step in range(max(steps - 2, 0), steps):
            for copy in stores(step):
                copy.wait()

    in_specs = [SCALARS, SPACE, LOCAL, LOCAL, LOCAL] + [SPACE] * len(arrays)
    args = [order, tokens, gain, scaled_cot, less, *arrays]
    aliases = {}
    if aliased:
        in_specs.append(SPACE)
        args.append(result)
        aliases = {len(args) - 1: 0}
    return pl.pallas_call(
        body,
        out_shape=jax.ShapeDtypeStruct((rows, width), BF16),
        in_specs=in_specs,
        out_specs=SPACE,
        input_output_aliases=aliases,
        scratch_shapes=[
            pltpu.VMEM((2, rows, 2 * depth), BF16),
            pltpu.VMEM((2, 2, depth, outs), BF16),
            pltpu.VMEM((2, rows, 2 * depth), BF16),
            pltpu.SemaphoreType.DMA((2, 2)),
            pltpu.SemaphoreType.DMA((2, 2)),
            pltpu.SemaphoreType.DMA((2, 2)),
        ],
        compiler_params=params(),
        cost_estimate=COST,
    )(*args)


def sums(groups, half, targets=()):
    terms = [term for halves_of in groups for items in halves_of for term in items]
    width = terms[0][0].shape[1]
    step = half // 2

    def view(array):
        return array.reshape(-1, half, width)

    def body(*refs):
        outs = refs[len(terms) :]
        k = 0
        for out, halves_of in zip(outs, groups):
            for part, items in enumerate(halves_of):
                total = refs[k][0].astype(F32)
                for j in range(1, len(items)):
                    total = total + refs[k + j][0].astype(F32)
                k += len(items)
                out[part] = total.astype(BF16)

    def term_spec(part):
        return pl.BlockSpec((1, step, width), lambda j: (part, j, 0))

    shapes = [
        (view(terms[targets[o]][0]).shape[0] if targets else len(halves_of), half, width)
        for o, halves_of in enumerate(groups)
    ]
    results = pl.pallas_call(
        body,
        out_shape=tuple(jax.ShapeDtypeStruct(shape, BF16) for shape in shapes),
        grid=(2,),
        in_specs=[term_spec(part) for _, part in terms],
        out_specs=tuple(
            pl.BlockSpec((len(halves_of), step, width), lambda j: (0, j, 0))
            for halves_of in groups
        ),
        input_output_aliases={term: o for o, term in enumerate(targets)},
        compiler_params=params(),
        cost_estimate=COST,
    )(*[view(array) for array, _ in terms])
    return [result.reshape(-1, width) for result in results]


def rearrange(sources, moves, shapes):
    def body(*refs):
        ins, outs = refs[: len(sources)], refs[len(sources) : len(sources) + len(shapes)]
        buf, in_sem, out_sem = refs[-3:]

        def load(k):
            i, start, n, _ = moves[k]
            return pltpu.make_async_copy(
                ins[i].at[pl.ds(start, n)], buf.at[k, pl.ds(0, n)], in_sem.at[k]
            )

        def stores(k):
            n, places = moves[k][2:]
            copies = []
            for j, (o, lead, first) in enumerate(places):
                target = outs[o] if lead is None else outs[o].at[lead]
                copies.append(
                    pltpu.make_async_copy(
                        buf.at[k, pl.ds(0, n)], target.at[pl.ds(first, n)], out_sem.at[k, j]
                    )
                )
            return copies

        for k in range(len(moves)):
            load(k).start()
        for k in range(len(moves)):
            load(k).wait()
            for copy in stores(k):
                copy.start()
        for k in range(len(moves)):
            for copy in stores(k):
                copy.wait()

    rows = max(n for _, _, n, _ in moves)
    return pl.pallas_call(
        body,
        out_shape=tuple(jax.ShapeDtypeStruct(shape, BF16) for shape in shapes),
        in_specs=[SPACE] * len(sources),
        out_specs=(SPACE,) * len(shapes),
        scratch_shapes=[
            pltpu.VMEM((len(moves), rows, sources[0].shape[1]), BF16),
            pltpu.SemaphoreType.DMA((len(moves),)),
            pltpu.SemaphoreType.DMA((len(moves), 3)),
        ],
        compiler_params=params(),
        cost_estimate=COST,
    )(*sources)


def after(values, *earlier):
    return lax.optimization_barrier((values, earlier))[0]


def per_device(
    tokens, gain, value_weight, cotangent, codes, scales, local_frag, momentum, global_frag
):
    groups = NX * NZ * NC
    gain_row = gain[None]
    own = value_weight[0]
    depth = own.shape[0]
    half = depth // 2
    early = halves((ZXP, ZXM, ZX2, ZZ))
    late = [(X2, 1), (XP, 0), (X2, 0), (XM, 1), (XP, 1), (XM, 0), (OWN, 0), (OWN, 1)]
    far_three = FAR[:-1]
    table = order_table(
        (
            (1, early + late),
            (0, early),
            (0, late),
            (0, NEAR),
            (1, NEAR),
            (0, far_three),
            (1, far_three),
            (0, FAR[-1:]),
            (1, FAR[-1:]),
        )
    )
    pair_count = len(early) // 2
    at_early, at_late, at_near = 4 * pair_count, 6 * pair_count, 8 * pair_count
    at_near_swap, at_far = at_near + len(NEAR), at_near + 2 * len(NEAR)
    at_last = at_far + 2 * len(far_three)

    xm = move(own, dx=1)
    xp = move(own, dx=-1)
    zz = move(own, dz=1)

    codes, local_frag = codes[0], local_frag[0]
    rows, frag_width = codes.shape
    blocks = scales.shape[2]
    delta = (
        (
            codes.astype(F32).reshape(rows, blocks, frag_width // blocks)
            * scales[0].astype(F32)[..., None]
        )
        .reshape(rows, frag_width)
        .astype(BF16)
    )
    me = lax.axis_index("rep")
    low, high, h = (me // NH) % 2, me // NH // 2, me % NH
    wide = frag_width // NY
    piece = wide // NH

    def cut(value, k, size):
        return lax.dynamic_slice_in_dim(value, k * size, size, axis=1)

    def low_half(bit):
        return jnp.concatenate(
            [cut(delta[:, : 2 * wide], bit, wide), cut(delta[:, 2 * wide :], bit, wide)], axis=1
        )

    kept, leaving = low_half(low), low_half(1 - low)
    got = swap_rep(leaving, y_bit=1)
    tokens_after, cot_after = after((tokens, cotangent), kept, leaving)
    rinv, scaled_cot = statistics(tokens_after, cot_after)
    kept, got = after((kept, got), scaled_cot)
    total = kept.astype(F32) + got.astype(F32)
    kept, leaving = cut(total, high, wide), cut(total, 1 - high, wide).astype(BF16)
    got = swap_rep(leaving, y_bit=2)
    sent_terms = weight_terms(
        tokens, gain_row, scaled_cot, (after(table, kept, leaving), 0, 2 * pair_count), groups
    )
    kept, got = after((kept, got), sent_terms)
    total = kept + got.astype(F32)
    kept, leaving = cut(total, h, piece), cut(total, 1 - h, piece).astype(BF16)

    xm, xp, zz = after((xm, xp, zz), sent_terms, leaving)
    near_shape = (len(NEAR), depth, own.shape[1])
    m_p, m_m, near = rearrange(
        (own, xp, xm, zz),
        (
            (2, 0, half, [(0, None, 0), (2, 2, 0)]),
            (1, half, half, [(1, None, 0), (2, 1, half)]),
            (3, 0, half, [(0, None, half), (1, None, half), (2, 3, 0)]),
            (3, half, half, [(0, None, depth), (1, None, depth), (2, 3, half)]),
            (2, half, half, [(2, 2, half)]),
            (1, 0, half, [(2, 1, 0)]),
            (0, 0, half, [(2, 0, 0)]),
            (0, half, half, [(2, 0, half)]),
        ),
        ((half + depth, near_shape[2]), (half + depth, near_shape[2]), near_shape),
    )
    r_p = move(m_p, dx=1)
    r_m = move(m_m, dx=-1)
    got_terms = move(after(sent_terms, m_p), dc=1)
    near_other = move(near, dc=1)
    near_list = [(near, k) for k in range(len(NEAR))]
    near_other_list = [(near_other, k) for k in range(len(NEAR))]
    partial = forward(tokens, gain_row, (table, at_near), near_list, None)

    p_zxp, p_zxm, p_zx2, p_zz = weight_terms(
        tokens, gain_row, scaled_cot, (after(table, partial), at_early, pair_count), groups,
        got_terms, 0,
    )
    c_x2 = move(p_zx2, dz=1)
    got = swap_rep(after(leaving, p_zx2), h_bit=1)
    partial = forward(
        tokens, gain_row, (after(table, p_zx2), at_near_swap), near_other_list, partial
    )
    kept, got = after((kept, got), partial)
    average = (kept + got.astype(F32)) / (NY * NH)
    new_momentum = 0.9 * momentum + average
    new_global = global_frag - 0.7 * (average + 0.9 * new_momentum)
    sent = new_global.astype(BF16)

    r_p, r_m, c_x2 = after((r_p, r_m, c_x2), sent)
    x2, far = rearrange(
        (r_p, r_m),
        (
            (0, 0, half, [(0, None, 0), (1, 0, 0)]),
            (1, 0, half, [(0, None, half), (1, 0, half)]),
            (1, half, depth, [(1, 1, 0)]),
            (0, half, depth, [(1, 2, 0)]),
        ),
        ((depth, own.shape[1]), (len(FAR) - 1, depth, own.shape[1])),
    )
    zx2 = move(x2, dz=1)
    far_other = move(far, dc=1)
    s_zxp, s_zxm = after((p_zxp, p_zxm), x2)
    a_p = move(s_zxp, dx=1)
    a_m = move(s_zxm, dx=-1)
    p_m1, p_m2, p_ends, p_own = weight_terms(
        tokens,
        gain_row,
        scaled_cot,
        (after(table, x2), at_late, pair_count),
        groups,
        got_terms,
        pair_count,
    )

    c_x2, p_m1, p_m2 = after((c_x2, p_m1, p_m2), p_own)
    m1, m2 = sums(
        ([[(p_m1, 0), (c_x2, 1)]], [[(p_m2, 0), (c_x2, 0)]]),
        half,
        (0, 2),
    )
    d1 = move(m1, dx=1)
    d2 = move(m2, dx=-1)
    far_list = [(far, k) for k in range(len(far_three))]
    far_other_list = [(far_other, k) for k in range(len(far_three))]
    partial = forward(
        tokens, gain_row, (after(table, m1, m2), at_far), far_list + far_other_list, partial
    )
    a_p, a_m, p_zz, zx2 = after((a_p, a_m, p_zz, zx2), partial)
    zx2_other = move(zx2, dc=1)
    (e_zz,) = sums(
        ([[(p_zz, 0), (a_p, 0), (a_m, 0)], [(p_zz, 1), (a_p, 1), (a_m, 1)]],),
        half,
    )
    f_z = move(e_zz, dz=1)
    got = swap_rep(after(sent, e_zz), h_bit=1)
    last_list = [(zx2, None), (zx2_other, None)]
    values, less = forward(
        tokens, gain_row, (after(table, e_zz), at_last), last_list, partial, (rinv, scaled_cot)
    )
    sent, got = after((sent, got), values)
    pair = jnp.where(
        h == 0, jnp.concatenate([sent, got], axis=1), jnp.concatenate([got, sent], axis=1)
    )
    got = swap_rep(pair, y_bit=2)

    def back(order, sources, result):
        return backward(tokens, gain_row, scaled_cot, less, order, sources, result)

    token_gradient = back(
        (after(table, pair), at_near), near_list + near_other_list, None
    )
    d1, d2, p_ends = after((d1, d2, p_ends), token_gradient)
    f1, f2 = sums(
        ([[(p_ends, 0), (d1, 0)]], [[(p_ends, 1), (d2, 0)]]), half
    )
    f_p = move(f1, dx=1)
    f_m = move(f2, dx=-1)
    pair, got = after((pair, got), f1, f2)
    quad = jnp.where(
        high == 0, jnp.concatenate([pair, got], axis=1), jnp.concatenate([got, pair], axis=1)
    )
    got = swap_rep(quad, y_bit=1)
    token_gradient = back(
        (after(table, quad), at_far), far_list + far_other_list + last_list, token_gradient
    )
    quad, got = after((quad, got), token_gradient)
    even, odd = jnp.where(low == 0, quad, got), jnp.where(low == 0, got, quad)
    full = jnp.concatenate(
        [even[:, :wide], odd[:, :wide], even[:, wide:], odd[:, wide:]], axis=1
    )
    merged = (0.5 * local_frag.astype(F32) + 0.5 * full.astype(F32)).astype(BF16)
    f_z, f_p, f_m, p_own = after((f_z, f_p, f_m, p_own), merged)
    (weight_grad,) = sums(
        (
            [
                [(p_own, 0), (d1, 1), (f_z, 0), (f_m, 0)],
                [(p_own, 1), (d2, 1), (f_z, 1), (f_p, 0)],
            ],
        ),
        half,
    )
    return (
        values,
        token_gradient,
        weight_grad[None],
        merged[None],
        new_momentum,
        new_global,
    )


def solution(mesh):
    return jax.shard_map(
        per_device,
        mesh=mesh,
        in_specs=(
            P(("rep", "fsdp"), None),
            P(),
            P("rep", "fsdp", None),
            P(("rep", "fsdp"), None),
            P("rep", "fsdp", None),
            P("rep", "fsdp", None),
            P("rep", "fsdp", None),
            P("fsdp", "rep"),
            P("fsdp", "rep"),
        ),
        out_specs=(
            P(("rep", "fsdp"), None),
            P(("rep", "fsdp"), None),
            P("rep", "fsdp", None),
            P("rep", "fsdp", None),
            P("fsdp", "rep"),
            P("fsdp", "rep"),
        ),
        check_vma=False,
    )
```

```python
import jax
import jax.numpy as jnp
from jax import lax
from jax.experimental import pallas as pl
from jax.experimental.pallas import tpu as pltpu
from jax.sharding import PartitionSpec as P

F32 = jnp.float32
BF16 = jnp.bfloat16
NX, NZ, NC, NY, NH = 4, 2, 2, 4, 2
OWN, XP, XM, ZZ = (0, 0), (1, 0), (3, 0), (0, 1)
X2, ZXP, ZXM, ZX2 = (2, 0), (1, 1), (3, 1), (2, 1)
NEAR = (OWN, XP, XM, ZZ)
FAR = (X2, ZXP, ZXM, ZX2)
VMEM = 62 * 2**20


def fsdp_index(x, z, c):
    return ((x % NX) * NZ + z % NZ) * NC + c % NC


def move(value, dx=0, dz=0, dc=0):
    pairs = [
        (fsdp_index(x, z, c), fsdp_index(x + dx, z + dz, c + dc))
        for x in range(NX)
        for z in range(NZ)
        for c in range(NC)
    ]
    return lax.ppermute(value, "fsdp", pairs)


def swap_rep(value, y_bit=0, h_bit=0):
    pairs = [(y * NH + h, (y ^ y_bit) * NH + (h ^ h_bit)) for y in range(NY) for h in range(NH)]
    return lax.ppermute(value, "rep", pairs)


def halves(places):
    return [(place, part) for place in places for part in (0, 1)]


def order_table(lists):
    me = lax.axis_index("fsdp")
    x, z, c = me // (NZ * NC), (me // NC) % NZ, me % NC
    table = []
    for dc, items in lists:
        for item in items:
            (dx, dz), part = item if isinstance(item[0], tuple) else (item, None)
            index = fsdp_index(x + dx, z + dz, c + dc)
            table.append(index if part is None else index * 2 + part)
    return jnp.stack(table).astype(jnp.int32)


def params():
    return pltpu.CompilerParams(vmem_limit_bytes=VMEM)


SPACE = pl.BlockSpec(memory_space=pltpu.HBM)
LOCAL = pl.BlockSpec(memory_space=pltpu.VMEM)
SCALARS = pl.BlockSpec(memory_space=pltpu.SMEM)
COST = pl.CostEstimate(flops=1, bytes_accessed=1, transcendentals=0)


def statistics(tokens, cotangent):
    rows, width = tokens.shape
    outs = cotangent.shape[1]
    parts = 8
    step = rows // parts

    def body(tok_ref, cot_ref, rinv_ref, scaled_ref, buf, sem):
        def load(k):
            return pltpu.make_async_copy(
                tok_ref.at[pl.ds(k * step, step)], buf.at[k], sem.at[k]
            )

        for k in range(parts):
            load(k).start()
        lanes = 512
        for k in range(parts):
            load(k).wait()
            total = jnp.zeros((step, lanes), F32)
            for first in range(0, width, lanes):
                value = buf[k, :, first : first + lanes].astype(F32)
                total = total + value * value
            mean = jnp.sum(total, axis=-1, keepdims=True) / width
            rinv = 1.0 / jnp.sqrt(mean + 1e-05)
            part = pl.ds(k * step, step)
            rinv_ref[part, :] = rinv
            scaled_ref[part, :] = (cot_ref[part, :].astype(F32) * rinv).astype(BF16)

    return pl.pallas_call(
        body,
        out_shape=(
            jax.ShapeDtypeStruct((rows, 1), F32),
            jax.ShapeDtypeStruct((rows, outs), BF16),
        ),
        in_specs=[SPACE, LOCAL],
        out_specs=(LOCAL, LOCAL),
        scratch_shapes=[
            pltpu.VMEM((parts, step, width), BF16),
            pltpu.SemaphoreType.DMA((parts,)),
        ],
        compiler_params=params(),
        cost_estimate=COST,
    )(tokens, cotangent)


def unit_columns(order_ref, k, unit):
    return pl.ds(pl.multiple_of(order_ref[k] * unit, unit), unit)


def token_copies(order_ref, base, tok_ref, buf, sem, step, unit, per):
    slot = step % 2
    return [
        pltpu.make_async_copy(
            tok_ref.at[:, unit_columns(order_ref, base + step * per + u, unit)],
            buf.at[slot, :, pl.ds(u * unit, unit)],
            sem.at[slot, u],
        )
        for u in range(per)
    ]


def unit_gain(order_ref, base, gain_ref, step, unit, per):
    return jnp.concatenate(
        [gain_ref[:, unit_columns(order_ref, base + step * per + u, unit)] for u in range(per)],
        axis=1,
    )


def weight_terms(tokens, gain, scaled_cot, order, groups, other=None, first=0):
    rows, width = tokens.shape
    outs = scaled_cot.shape[1]
    unit = width // (NX * NZ * NC * 2)
    order, base, count = order
    depth = 2 * unit
    steps = count // 2

    def body(order_ref, tok_ref, gain_ref, cot_ref, *rest):
        if other is None:
            out_ref, tok_buf, out_buf, tok_sem, out_sem = rest
            targets = [out_ref.at[k] for k in range(count)]
        else:
            other_ref, targets = rest[0], rest[1 : 1 + count]
            tok_buf, out_buf, tok_sem, out_sem, other_buf, other_sem = rest[1 + count :]

        def loads(step):
            copies = token_copies(order_ref, base, tok_ref, tok_buf, tok_sem, step, unit, 4)
            if other is not None:
                copies += [
                    pltpu.make_async_copy(
                        other_ref.at[first + 2 * step + j],
                        other_buf.at[step % 2, j],
                        other_sem.at[step % 2, j],
                    )
                    for j in range(2)
                ]
            return copies

        def stores(step):
            return [
                pltpu.make_async_copy(
                    out_buf.at[step % 2, j], targets[2 * step + j], out_sem.at[step % 2, j]
                )
                for j in range(2)
            ]

        for copy in loads(0):
            copy.start()
        for step in range(steps):
            slot = step % 2
            if step + 1 < steps:
                for copy in loads(step + 1):
                    copy.start()
            for copy in loads(step):
                copy.wait()
            gains = unit_gain(order_ref, base, gain_ref, step, unit, 4)
            if step >= 2:
                for copy in stores(step - 2):
                    copy.wait()
            for j in range(2):
                for row in range(0, depth, unit):
                    start = j * depth + row
                    left = (
                        tok_buf[slot, :, pl.ds(start, unit)].astype(F32)
                        * gains[:, start : start + unit]
                    ).astype(BF16)
                    term = lax.dot_general(
                        left, cot_ref[...], (((0,), (0,)), ((), ())), preferred_element_type=F32
                    ) * (1.0 / groups)
                    if other is not None:
                        term = term + other_buf[slot, j, pl.ds(row, unit), :].astype(F32)
                    out_buf[slot, j, pl.ds(row, unit), :] = term.astype(BF16)
            for copy in stores(step):
                copy.start()
        for step in range(max(steps - 2, 0), steps):
            for copy in stores(step):
                copy.wait()

    scratch = [
        pltpu.VMEM((2, rows, 2 * depth), BF16),
        pltpu.VMEM((2, 2, depth, outs), BF16),
        pltpu.SemaphoreType.DMA((2, 4)),
        pltpu.SemaphoreType.DMA((2, 2)),
    ]
    in_specs, args = [SCALARS, SPACE, LOCAL, LOCAL], [order, tokens, gain, scaled_cot]
    if other is None:
        out_shape, out_specs = jax.ShapeDtypeStruct((count, depth, outs), BF16), SPACE
    else:
        out_shape = (jax.ShapeDtypeStruct((depth, outs), BF16),) * count
        out_specs = (SPACE,) * count
        in_specs.append(SPACE)
        args.append(other)
        scratch += [pltpu.VMEM((2, 2, depth, outs), BF16), pltpu.SemaphoreType.DMA((2, 2))]
    return pl.pallas_call(
        body,
        out_shape=out_shape,
        in_specs=in_specs,
        out_specs=out_specs,
        scratch_shapes=scratch,
        compiler_params=params(),
        cost_estimate=COST,
    )(*args)


def unique(sources):
    arrays, places = [], []
    for array, where in sources:
        position = next((i for i, known in enumerate(arrays) if known is array), len(arrays))
        if position == len(arrays):
            arrays.append(array)
        places.append((position, where))
    return arrays, places


def weight_copies(refs, places, buf, sem, step):
    copies = []
    for j in range(2):
        position, where = places[2 * step + j]
        source = refs[position] if where is None else refs[position].at[where]
        copies.append(pltpu.make_async_copy(source, buf.at[step % 2, j], sem.at[step % 2, j]))
    return copies


def forward(tokens, gain, order, sources, total, last=None):
    rows, width = tokens.shape
    arrays, places = unique(sources)
    depth, outs = arrays[0].shape[-2:]
    steps, ins = len(places) // 2, len(arrays)
    order, base = order
    rest_in = (0 if total is None else 1) + (0 if last is None else 2)

    def body(order_ref, tok_ref, gain_ref, *rest):
        extra = rest[ins : ins + rest_in]
        results = rest[ins + rest_in : -4]
        tok_buf, w_buf, tok_sem, w_sem = rest[-4:]

        def loads(step):
            return token_copies(
                order_ref, base, tok_ref, tok_buf, tok_sem, step, depth, 2
            ) + weight_copies(rest[:ins], places, w_buf, w_sem, step)

        for copy in loads(0):
            copy.start()
        acc = None if total is None else extra[0][...]
        for step in range(steps):
            if step + 1 < steps:
                for copy in loads(step + 1):
                    copy.start()
            for copy in loads(step):
                copy.wait()
            gains = unit_gain(order_ref, base, gain_ref, step, depth, 2)
            left = (tok_buf[step % 2].astype(F32) * gains).astype(BF16)
            term = jnp.dot(
                left, w_buf[step % 2].reshape(2 * depth, outs), preferred_element_type=F32
            )
            acc = term if acc is None else acc + term
        if last is None:
            results[0][...] = acc
        else:
            rinv = extra[-2][...]
            results[0][...] = (acc * rinv).astype(BF16)
            dots = jnp.sum(acc * extra[-1][...].astype(F32), axis=-1, keepdims=True)
            results[1][...] = dots * rinv * rinv * (1.0 / width)

    if last is None:
        out_shape, out_specs = jax.ShapeDtypeStruct((rows, outs), F32), LOCAL
    else:
        out_shape = (
            jax.ShapeDtypeStruct((rows, outs), BF16),
            jax.ShapeDtypeStruct((rows, 1), F32),
        )
        out_specs = (LOCAL, LOCAL)
    return pl.pallas_call(
        body,
        out_shape=out_shape,
        in_specs=[SCALARS, SPACE, LOCAL] + [SPACE] * ins + [LOCAL] * rest_in,
        out_specs=out_specs,
        scratch_shapes=[
            pltpu.VMEM((2, rows, 2 * depth), BF16),
            pltpu.VMEM((2, 2, depth, outs), BF16),
            pltpu.SemaphoreType.DMA((2, 2)),
            pltpu.SemaphoreType.DMA((2, 2)),
        ],
        compiler_params=params(),
        cost_estimate=COST,
    )(order, tokens, gain, *arrays, *(() if total is None else (total,)), *(last or ()))


def backward(tokens, gain, scaled_cot, less, order, sources, result):
    rows, width = tokens.shape
    arrays, places = unique(sources)
    depth, outs = arrays[0].shape[-2:]
    steps = len(places) // 2
    order, base = order
    aliased = result is not None

    def body(order_ref, tok_ref, gain_ref, cot_ref, less_ref, *rest):
        refs = rest[: len(arrays)]
        out_ref, tok_buf, w_buf, out_buf, tok_sem, w_sem, out_sem = rest[-7:]

        def loads(step):
            return token_copies(
                order_ref, base, tok_ref, tok_buf, tok_sem, step, depth, 2
            ) + weight_copies(refs, places, w_buf, w_sem, step)

        def stores(step):
            return [
                pltpu.make_async_copy(
                    out_buf.at[step % 2, :, pl.ds(u * depth, depth)],
                    out_ref.at[:, unit_columns(order_ref, base + step * 2 + u, depth)],
                    out_sem.at[step % 2, u],
                )
                for u in range(2)
            ]

        for copy in loads(0):
            copy.start()
        for step in range(steps):
            slot = step % 2
            if step + 1 < steps:
                for copy in loads(step + 1):
                    copy.start()
            for copy in loads(step):
                copy.wait()
            gains = unit_gain(order_ref, base, gain_ref, step, depth, 2)
            if step >= 2:
                for copy in stores(step - 2):
                    copy.wait()
            for j in range(2):
                for first in range(0, depth, depth // 2):
                    part = pl.ds(j * depth + first, depth // 2)
                    back = lax.dot_general(
                        cot_ref[...],
                        w_buf[slot, j, pl.ds(first, depth // 2), :],
                        (((1,), (1,)), ((), ())),
                        preferred_element_type=F32,
                    )
                    gain_part = gains[:, j * depth + first : j * depth + first + depth // 2]
                    out_buf[slot, :, part] = (
                        back * gain_part - tok_buf[slot, :, part].astype(F32) * less_ref[...]
                    ).astype(BF16)
            for copy in stores(step):
                copy.start()
        for step in range(max(steps - 2, 0), steps):
            for copy in stores(step):
                copy.wait()

    in_specs = [SCALARS, SPACE, LOCAL, LOCAL, LOCAL] + [SPACE] * len(arrays)
    args = [order, tokens, gain, scaled_cot, less, *arrays]
    aliases = {}
    if aliased:
        in_specs.append(SPACE)
        args.append(result)
        aliases = {len(args) - 1: 0}
    return pl.pallas_call(
        body,
        out_shape=jax.ShapeDtypeStruct((rows, width), BF16),
        in_specs=in_specs,
        out_specs=SPACE,
        input_output_aliases=aliases,
        scratch_shapes=[
            pltpu.VMEM((2, rows, 2 * depth), BF16),
            pltpu.VMEM((2, 2, depth, outs), BF16),
            pltpu.VMEM((2, rows, 2 * depth), BF16),
            pltpu.SemaphoreType.DMA((2, 2)),
            pltpu.SemaphoreType.DMA((2, 2)),
            pltpu.SemaphoreType.DMA((2, 2)),
        ],
        compiler_params=params(),
        cost_estimate=COST,
    )(*args)


def sums(groups, half, targets=()):
    terms = [term for halves_of in groups for items in halves_of for term in items]
    width = terms[0][0].shape[1]
    step = half // 2

    def view(array):
        return array.reshape(-1, half, width)

    def body(*refs):
        outs = refs[len(terms) :]
        k = 0
        for out, halves_of in zip(outs, groups):
            for part, items in enumerate(halves_of):
                total = refs[k][0].astype(F32)
                for j in range(1, len(items)):
                    total = total + refs[k + j][0].astype(F32)
                k += len(items)
                out[part] = total.astype(BF16)

    def term_spec(part):
        return pl.BlockSpec((1, step, width), lambda j: (part, j, 0))

    shapes = [
        (view(terms[targets[o]][0]).shape[0] if targets else len(halves_of), half, width)
        for o, halves_of in enumerate(groups)
    ]
    results = pl.pallas_call(
        body,
        out_shape=tuple(jax.ShapeDtypeStruct(shape, BF16) for shape in shapes),
        grid=(2,),
        in_specs=[term_spec(part) for _, part in terms],
        out_specs=tuple(
            pl.BlockSpec((len(halves_of), step, width), lambda j: (0, j, 0))
            for halves_of in groups
        ),
        input_output_aliases={term: o for o, term in enumerate(targets)},
        compiler_params=params(),
        cost_estimate=COST,
    )(*[view(array) for array, _ in terms])
    return [result.reshape(-1, width) for result in results]


def rearrange(sources, moves, shapes):
    def body(*refs):
        ins, outs = refs[: len(sources)], refs[len(sources) : len(sources) + len(shapes)]
        buf, in_sem, out_sem = refs[-3:]

        def load(k):
            i, start, n, _ = moves[k]
            return pltpu.make_async_copy(
                ins[i].at[pl.ds(start, n)], buf.at[k, pl.ds(0, n)], in_sem.at[k]
            )

        def stores(k):
            n, places = moves[k][2:]
            copies = []
            for j, (o, lead, first) in enumerate(places):
                target = outs[o] if lead is None else outs[o].at[lead]
                copies.append(
                    pltpu.make_async_copy(
                        buf.at[k, pl.ds(0, n)], target.at[pl.ds(first, n)], out_sem.at[k, j]
                    )
                )
            return copies

        for k in range(len(moves)):
            load(k).start()
        for k in range(len(moves)):
            load(k).wait()
            for copy in stores(k):
                copy.start()
        for k in range(len(moves)):
            for copy in stores(k):
                copy.wait()

    rows = max(n for _, _, n, _ in moves)
    return pl.pallas_call(
        body,
        out_shape=tuple(jax.ShapeDtypeStruct(shape, BF16) for shape in shapes),
        in_specs=[SPACE] * len(sources),
        out_specs=(SPACE,) * len(shapes),
        scratch_shapes=[
            pltpu.VMEM((len(moves), rows, sources[0].shape[1]), BF16),
            pltpu.SemaphoreType.DMA((len(moves),)),
            pltpu.SemaphoreType.DMA((len(moves), 3)),
        ],
        compiler_params=params(),
        cost_estimate=COST,
    )(*sources)


def after(values, *earlier):
    return lax.optimization_barrier((values, earlier))[0]


def per_device(
    tokens, gain, value_weight, cotangent, codes, scales, local_frag, momentum, global_frag
):
    groups = NX * NZ * NC
    gain_row = gain[None]
    own = value_weight[0]
    depth = own.shape[0]
    half = depth // 2
    early = halves((ZX2, ZZ, ZXP, ZXM))
    late = [(X2, 1), (XP, 0), (X2, 0), (XM, 1), (XP, 1), (XM, 0), (OWN, 0), (OWN, 1)]
    far_three = FAR[:-1]
    table = order_table(
        (
            (1, early + late),
            (0, early),
            (0, late),
            (0, NEAR),
            (1, NEAR),
            (0, far_three),
            (1, far_three),
            (0, FAR[-1:]),
            (1, FAR[-1:]),
        )
    )
    pair_count = len(early) // 2
    at_early, at_late, at_near = 4 * pair_count, 6 * pair_count, 8 * pair_count
    at_near_swap, at_far = at_near + len(NEAR), at_near + 2 * len(NEAR)
    at_last = at_far + 2 * len(far_three)

    xm = move(own, dx=1)
    xp = move(own, dx=-1)
    zz = move(own, dz=1)

    codes, local_frag = codes[0], local_frag[0]
    rows, frag_width = codes.shape
    blocks = scales.shape[2]
    delta = (
        (
            codes.astype(F32).reshape(rows, blocks, frag_width // blocks)
            * scales[0].astype(F32)[..., None]
        )
        .reshape(rows, frag_width)
        .astype(BF16)
    )
    me = lax.axis_index("rep")
    low, high, h = (me // NH) % 2, me // NH // 2, me % NH
    wide = frag_width // NY
    piece = wide // NH

    def cut(value, k, size):
        return lax.dynamic_slice_in_dim(value, k * size, size, axis=1)

    def low_half(bit):
        return jnp.concatenate(
            [cut(delta[:, : 2 * wide], bit, wide), cut(delta[:, 2 * wide :], bit, wide)], axis=1
        )

    kept, leaving = low_half(low), low_half(1 - low)
    got = swap_rep(leaving, y_bit=1)
    tokens_after, cot_after = after((tokens, cotangent), kept, leaving)
    rinv, scaled_cot = statistics(tokens_after, cot_after)
    sent_terms = weight_terms(
        tokens, gain_row, scaled_cot, (table, 0, 2 * pair_count), groups
    )

    kept, got = after((kept, got), sent_terms)
    total = kept.astype(F32) + got.astype(F32)
    kept, leaving = cut(total, high, wide), cut(total, 1 - high, wide).astype(BF16)
    got = swap_rep(leaving, y_bit=2)

    xm, xp, zz = after((xm, xp, zz), sent_terms, kept, leaving)
    near_shape = (len(NEAR), depth, own.shape[1])
    m_p, m_m, near = rearrange(
        (own, xp, xm, zz),
        (
            (2, 0, half, [(0, None, 0), (2, 2, 0)]),
            (1, half, half, [(1, None, 0), (2, 1, half)]),
            (3, 0, half, [(0, None, half), (1, None, half), (2, 3, 0)]),
            (3, half, half, [(0, None, depth), (1, None, depth), (2, 3, half)]),
            (2, half, half, [(2, 2, half)]),
            (1, 0, half, [(2, 1, 0)]),
            (0, 0, half, [(2, 0, 0)]),
            (0, half, half, [(2, 0, half)]),
        ),
        ((half + depth, near_shape[2]), (half + depth, near_shape[2]), near_shape),
    )
    r_p = move(m_p, dx=1)
    r_m = move(m_m, dx=-1)
    got_terms = move(after(sent_terms, m_p), dc=1)
    near_other = move(near, dc=1)
    near_list = [(near, k) for k in range(len(NEAR))]
    near_other_list = [(near_other, k) for k in range(len(NEAR))]

    partial = forward(
        tokens, gain_row, (table, at_near), near_list, None
    )
    p_zx2, p_zz = weight_terms(
        tokens, gain_row, scaled_cot, (after(table, partial), at_early, 2), groups,
        got_terms, 0,
    )
    c_x2 = move(p_zx2, dz=1)
    p_zxp, p_zxm = weight_terms(
        tokens, gain_row, scaled_cot, (after(table, p_zx2), at_early + 4, 2), groups,
        got_terms, 2,
    )
    kept, got = after((kept, got), p_zxp)
    total = kept + got.astype(F32)
    kept, leaving = cut(total, h, piece), cut(total, 1 - h, piece).astype(BF16)
    partial = forward(
        tokens, gain_row, (after(table, kept, leaving), at_near_swap), near_other_list, partial
    )
    r_p, r_m, c_x2 = after((r_p, r_m, c_x2), partial)
    x2, far = rearrange(
        (r_p, r_m),
        (
            (0, 0, half, [(0, None, 0), (1, 0, 0)]),
            (1, 0, half, [(0, None, half), (1, 0, half)]),
            (1, half, depth, [(1, 1, 0)]),
            (0, half, depth, [(1, 2, 0)]),
        ),
        ((depth, own.shape[1]), (len(FAR) - 1, depth, own.shape[1])),
    )
    zx2 = move(x2, dz=1)
    got = swap_rep(after(leaving, x2), h_bit=1)
    far_other = move(far, dc=1)
    s_zxp, s_zxm = after((p_zxp, p_zxm), x2)
    a_p = move(s_zxp, dx=1)
    a_m = move(s_zxm, dx=-1)
    p_m1, p_m2, p_ends, p_own = weight_terms(
        tokens,
        gain_row,
        scaled_cot,
        (after(table, x2), at_late, pair_count),
        groups,
        got_terms,
        pair_count,
    )

    c_x2, p_m1, p_m2 = after((c_x2, p_m1, p_m2), p_own)
    m1, m2 = sums(
        ([[(p_m1, 0), (c_x2, 1)]], [[(p_m2, 0), (c_x2, 0)]]),
        half,
        (0, 2),
    )
    d1 = move(m1, dx=1)
    d2 = move(m2, dx=-1)
    far_list = [(far, k) for k in range(len(far_three))]
    far_other_list = [(far_other, k) for k in range(len(far_three))]
    partial = forward(
        tokens, gain_row, (after(table, m1, m2), at_far), far_list + far_other_list, partial
    )
    a_p, a_m, p_zz, zx2, kept, got = after((a_p, a_m, p_zz, zx2, kept, got), partial)
    average = (kept + got.astype(F32)) / (NY * NH)
    new_momentum = 0.9 * momentum + average
    new_global = global_frag - 0.7 * (average + 0.9 * new_momentum)
    sent = new_global.astype(BF16)

    zx2_other = move(zx2, dc=1)
    (e_zz,) = sums(
        ([[(p_zz, 0), (a_p, 0), (a_m, 0)], [(p_zz, 1), (a_p, 1), (a_m, 1)]],),
        half,
    )
    f_z = move(e_zz, dz=1)
    got = swap_rep(after(sent, e_zz), h_bit=1)
    last_list = [(zx2, None), (zx2_other, None)]
    values, less = forward(
        tokens, gain_row, (after(table, e_zz), at_last), last_list, partial, (rinv, scaled_cot)
    )
    sent, got = after((sent, got), values)
    pair = jnp.where(
        h == 0, jnp.concatenate([sent, got], axis=1), jnp.concatenate([got, sent], axis=1)
    )
    got = swap_rep(pair, y_bit=2)

    def back(order, sources, result):
        return backward(tokens, gain_row, scaled_cot, less, order, sources, result)

    token_gradient = back(
        (after(table, pair), at_near), near_list + near_other_list, None
    )
    d1, d2, p_ends = after((d1, d2, p_ends), token_gradient)
    f1, f2 = sums(
        ([[(p_ends, 0), (d1, 0)]], [[(p_ends, 1), (d2, 0)]]), half
    )
    f_p = move(f1, dx=1)
    f_m = move(f2, dx=-1)
    pair, got = after((pair, got), f1, f2)
    quad = jnp.where(
        high == 0, jnp.concatenate([pair, got], axis=1), jnp.concatenate([got, pair], axis=1)
    )
    got = swap_rep(quad, y_bit=1)
    token_gradient = back(
        (after(table, quad), at_far), far_list + far_other_list + last_list, token_gradient
    )
    quad, got = after((quad, got), token_gradient)
    even, odd = jnp.where(low == 0, quad, got), jnp.where(low == 0, got, quad)
    full = jnp.concatenate(
        [even[:, :wide], odd[:, :wide], even[:, wide:], odd[:, wide:]], axis=1
    )
    merged = (0.5 * local_frag.astype(F32) + 0.5 * full.astype(F32)).astype(BF16)
    f_z, f_p, f_m, p_own = after((f_z, f_p, f_m, p_own), merged)
    (weight_grad,) = sums(
        (
            [
                [(p_own, 0), (d1, 1), (f_z, 0), (f_m, 0)],
                [(p_own, 1), (d2, 1), (f_z, 1), (f_p, 0)],
            ],
        ),
        half,
    )
    return (
        values,
        token_gradient,
        weight_grad[None],
        merged[None],
        new_momentum,
        new_global,
    )


def solution(mesh):
    return jax.shard_map(
        per_device,
        mesh=mesh,
        in_specs=(
            P(("rep", "fsdp"), None),
            P(),
            P("rep", "fsdp", None),
            P(("rep", "fsdp"), None),
            P("rep", "fsdp", None),
            P("rep", "fsdp", None),
            P("rep", "fsdp", None),
            P("fsdp", "rep"),
            P("fsdp", "rep"),
        ),
        out_specs=(
            P(("rep", "fsdp"), None),
            P(("rep", "fsdp"), None),
            P("rep", "fsdp", None),
            P("rep", "fsdp", None),
            P("fsdp", "rep"),
            P("fsdp", "rep"),
        ),
        check_vma=False,
    )
```

```python
import jax
import jax.numpy as jnp
from jax import lax
from jax.experimental import pallas as pl
from jax.experimental.pallas import tpu as pltpu
from jax.sharding import PartitionSpec as P

F32 = jnp.float32
BF16 = jnp.bfloat16
NX, NZ, NC, NY, NH = 4, 2, 2, 4, 2
OWN, XP, XM, ZZ = (0, 0), (1, 0), (3, 0), (0, 1)
X2, ZXP, ZXM, ZX2 = (2, 0), (1, 1), (3, 1), (2, 1)
NEAR = (OWN, XP, XM, ZZ)
FAR = (X2, ZXP, ZXM, ZX2)
VMEM = 62 * 2**20


def fsdp_index(x, z, c):
    return ((x % NX) * NZ + z % NZ) * NC + c % NC


def move(value, dx=0, dz=0, dc=0):
    pairs = [
        (fsdp_index(x, z, c), fsdp_index(x + dx, z + dz, c + dc))
        for x in range(NX)
        for z in range(NZ)
        for c in range(NC)
    ]
    return lax.ppermute(value, "fsdp", pairs)


def swap_rep(value, y_bit=0, h_bit=0):
    pairs = [(y * NH + h, (y ^ y_bit) * NH + (h ^ h_bit)) for y in range(NY) for h in range(NH)]
    return lax.ppermute(value, "rep", pairs)


def halves(places):
    return [(place, part) for place in places for part in (0, 1)]


def order_table(lists):
    me = lax.axis_index("fsdp")
    x, z, c = me // (NZ * NC), (me // NC) % NZ, me % NC
    table = []
    for dc, items in lists:
        for item in items:
            (dx, dz), part = item if isinstance(item[0], tuple) else (item, None)
            index = fsdp_index(x + dx, z + dz, c + dc)
            table.append(index if part is None else index * 2 + part)
    return jnp.stack(table).astype(jnp.int32)


def params():
    return pltpu.CompilerParams(vmem_limit_bytes=VMEM)


SPACE = pl.BlockSpec(memory_space=pltpu.HBM)
LOCAL = pl.BlockSpec(memory_space=pltpu.VMEM)
SCALARS = pl.BlockSpec(memory_space=pltpu.SMEM)
COST = pl.CostEstimate(flops=1, bytes_accessed=1, transcendentals=0)


def statistics(tokens, cotangent):
    rows, width = tokens.shape
    outs = cotangent.shape[1]
    parts = 8
    step = rows // parts

    def body(tok_ref, cot_ref, rinv_ref, scaled_ref, buf, sem):
        def load(k):
            return pltpu.make_async_copy(
                tok_ref.at[pl.ds(k * step, step)], buf.at[k], sem.at[k]
            )

        for k in range(parts):
            load(k).start()
        lanes = 512
        for k in range(parts):
            load(k).wait()
            total = jnp.zeros((step, lanes), F32)
            for first in range(0, width, lanes):
                value = buf[k, :, first : first + lanes].astype(F32)
                total = total + value * value
            mean = jnp.sum(total, axis=-1, keepdims=True) / width
            rinv = 1.0 / jnp.sqrt(mean + 1e-05)
            part = pl.ds(k * step, step)
            rinv_ref[part, :] = rinv
            scaled_ref[part, :] = (cot_ref[part, :].astype(F32) * rinv).astype(BF16)

    return pl.pallas_call(
        body,
        out_shape=(
            jax.ShapeDtypeStruct((rows, 1), F32),
            jax.ShapeDtypeStruct((rows, outs), BF16),
        ),
        in_specs=[SPACE, LOCAL],
        out_specs=(LOCAL, LOCAL),
        scratch_shapes=[
            pltpu.VMEM((parts, step, width), BF16),
            pltpu.SemaphoreType.DMA((parts,)),
        ],
        compiler_params=params(),
        cost_estimate=COST,
    )(tokens, cotangent)


def unit_columns(order_ref, k, unit):
    return pl.ds(pl.multiple_of(order_ref[k] * unit, unit), unit)


def token_copies(order_ref, base, tok_ref, buf, sem, step, unit, per):
    slot = step % 2
    return [
        pltpu.make_async_copy(
            tok_ref.at[:, unit_columns(order_ref, base + step * per + u, unit)],
            buf.at[slot, :, pl.ds(u * unit, unit)],
            sem.at[slot, u],
        )
        for u in range(per)
    ]


def unit_gain(order_ref, base, gain_ref, step, unit, per):
    return jnp.concatenate(
        [gain_ref[:, unit_columns(order_ref, base + step * per + u, unit)] for u in range(per)],
        axis=1,
    )


def weight_terms(tokens, gain, scaled_cot, order, groups, other=None, first=0):
    rows, width = tokens.shape
    outs = scaled_cot.shape[1]
    unit = width // (NX * NZ * NC * 2)
    order, base, count = order
    depth = 2 * unit
    steps = count // 2

    def body(order_ref, tok_ref, gain_ref, cot_ref, *rest):
        if other is None:
            *out_refs, tok_buf, out_buf, tok_sem, out_sem = rest
            targets = [ref.at[k] for ref in out_refs for k in range(count // 2)]
        else:
            other_ref, targets = rest[0], rest[1 : 1 + count]
            tok_buf, out_buf, tok_sem, out_sem, other_buf, other_sem = rest[1 + count :]

        def loads(step):
            copies = token_copies(order_ref, base, tok_ref, tok_buf, tok_sem, step, unit, 4)
            if other is not None:
                copies += [
                    pltpu.make_async_copy(
                        other_ref.at[first + 2 * step + j],
                        other_buf.at[step % 2, j],
                        other_sem.at[step % 2, j],
                    )
                    for j in range(2)
                ]
            return copies

        def stores(step):
            return [
                pltpu.make_async_copy(
                    out_buf.at[step % 2, j], targets[2 * step + j], out_sem.at[step % 2, j]
                )
                for j in range(2)
            ]

        for copy in loads(0):
            copy.start()
        for step in range(steps):
            slot = step % 2
            if step + 1 < steps:
                for copy in loads(step + 1):
                    copy.start()
            for copy in loads(step):
                copy.wait()
            gains = unit_gain(order_ref, base, gain_ref, step, unit, 4)
            if step >= 2:
                for copy in stores(step - 2):
                    copy.wait()
            for j in range(2):
                for row in range(0, depth, unit):
                    start = j * depth + row
                    left = (
                        tok_buf[slot, :, pl.ds(start, unit)].astype(F32)
                        * gains[:, start : start + unit]
                    ).astype(BF16)
                    term = lax.dot_general(
                        left, cot_ref[...], (((0,), (0,)), ((), ())), preferred_element_type=F32
                    ) * (1.0 / groups)
                    if other is not None:
                        term = term + other_buf[slot, j, pl.ds(row, unit), :].astype(F32)
                    out_buf[slot, j, pl.ds(row, unit), :] = term.astype(BF16)
            for copy in stores(step):
                copy.start()
        for step in range(max(steps - 2, 0), steps):
            for copy in stores(step):
                copy.wait()

    scratch = [
        pltpu.VMEM((2, rows, 2 * depth), BF16),
        pltpu.VMEM((2, 2, depth, outs), BF16),
        pltpu.SemaphoreType.DMA((2, 4)),
        pltpu.SemaphoreType.DMA((2, 2)),
    ]
    in_specs, args = [SCALARS, SPACE, LOCAL, LOCAL], [order, tokens, gain, scaled_cot]
    if other is None:
        out_shape = (jax.ShapeDtypeStruct((count // 2, depth, outs), BF16),) * 2
        out_specs = (SPACE,) * 2
    else:
        out_shape = (jax.ShapeDtypeStruct((depth, outs), BF16),) * count
        out_specs = (SPACE,) * count
        in_specs.append(SPACE)
        args.append(other)
        scratch += [pltpu.VMEM((2, 2, depth, outs), BF16), pltpu.SemaphoreType.DMA((2, 2))]
    return pl.pallas_call(
        body,
        out_shape=out_shape,
        in_specs=in_specs,
        out_specs=out_specs,
        scratch_shapes=scratch,
        compiler_params=params(),
        cost_estimate=COST,
    )(*args)


def unique(sources):
    arrays, places = [], []
    for array, where in sources:
        position = next((i for i, known in enumerate(arrays) if known is array), len(arrays))
        if position == len(arrays):
            arrays.append(array)
        places.append((position, where))
    return arrays, places


def weight_copies(refs, places, buf, sem, step):
    copies = []
    for j in range(2):
        position, where = places[2 * step + j]
        source = refs[position] if where is None else refs[position].at[where]
        copies.append(pltpu.make_async_copy(source, buf.at[step % 2, j], sem.at[step % 2, j]))
    return copies


def forward(tokens, gain, order, sources, total, last=None):
    rows, width = tokens.shape
    arrays, places = unique(sources)
    depth, outs = arrays[0].shape[-2:]
    steps, ins = len(places) // 2, len(arrays)
    order, base = order
    rest_in = (0 if total is None else 1) + (0 if last is None else 2)

    def body(order_ref, tok_ref, gain_ref, *rest):
        extra = rest[ins : ins + rest_in]
        results = rest[ins + rest_in : -4]
        tok_buf, w_buf, tok_sem, w_sem = rest[-4:]

        def loads(step):
            return token_copies(
                order_ref, base, tok_ref, tok_buf, tok_sem, step, depth, 2
            ) + weight_copies(rest[:ins], places, w_buf, w_sem, step)

        for copy in loads(0):
            copy.start()
        acc = None if total is None else extra[0][...]
        for step in range(steps):
            if step + 1 < steps:
                for copy in loads(step + 1):
                    copy.start()
            for copy in loads(step):
                copy.wait()
            gains = unit_gain(order_ref, base, gain_ref, step, depth, 2)
            left = (tok_buf[step % 2].astype(F32) * gains).astype(BF16)
            term = jnp.dot(
                left, w_buf[step % 2].reshape(2 * depth, outs), preferred_element_type=F32
            )
            acc = term if acc is None else acc + term
        if last is None:
            results[0][...] = acc
        else:
            rinv = extra[-2][...]
            results[0][...] = (acc * rinv).astype(BF16)
            dots = jnp.sum(acc * extra[-1][...].astype(F32), axis=-1, keepdims=True)
            results[1][...] = dots * rinv * rinv * (1.0 / width)

    if last is None:
        out_shape, out_specs = jax.ShapeDtypeStruct((rows, outs), F32), LOCAL
    else:
        out_shape = (
            jax.ShapeDtypeStruct((rows, outs), BF16),
            jax.ShapeDtypeStruct((rows, 1), F32),
        )
        out_specs = (LOCAL, LOCAL)
    return pl.pallas_call(
        body,
        out_shape=out_shape,
        in_specs=[SCALARS, SPACE, LOCAL] + [SPACE] * ins + [LOCAL] * rest_in,
        out_specs=out_specs,
        scratch_shapes=[
            pltpu.VMEM((2, rows, 2 * depth), BF16),
            pltpu.VMEM((2, 2, depth, outs), BF16),
            pltpu.SemaphoreType.DMA((2, 2)),
            pltpu.SemaphoreType.DMA((2, 2)),
        ],
        compiler_params=params(),
        cost_estimate=COST,
    )(order, tokens, gain, *arrays, *(() if total is None else (total,)), *(last or ()))


def backward(tokens, gain, scaled_cot, less, order, sources, result):
    rows, width = tokens.shape
    arrays, places = unique(sources)
    depth, outs = arrays[0].shape[-2:]
    steps = len(places) // 2
    order, base = order
    aliased = result is not None

    def body(order_ref, tok_ref, gain_ref, cot_ref, less_ref, *rest):
        refs = rest[: len(arrays)]
        out_ref, tok_buf, w_buf, out_buf, tok_sem, w_sem, out_sem = rest[-7:]

        def loads(step):
            return token_copies(
                order_ref, base, tok_ref, tok_buf, tok_sem, step, depth, 2
            ) + weight_copies(refs, places, w_buf, w_sem, step)

        def stores(step):
            return [
                pltpu.make_async_copy(
                    out_buf.at[step % 2, :, pl.ds(u * depth, depth)],
                    out_ref.at[:, unit_columns(order_ref, base + step * 2 + u, depth)],
                    out_sem.at[step % 2, u],
                )
                for u in range(2)
            ]

        for copy in loads(0):
            copy.start()
        for step in range(steps):
            slot = step % 2
            if step + 1 < steps:
                for copy in loads(step + 1):
                    copy.start()
            for copy in loads(step):
                copy.wait()
            gains = unit_gain(order_ref, base, gain_ref, step, depth, 2)
            if step >= 2:
                for copy in stores(step - 2):
                    copy.wait()
            for j in range(2):
                for first in range(0, depth, depth // 2):
                    part = pl.ds(j * depth + first, depth // 2)
                    back = lax.dot_general(
                        cot_ref[...],
                        w_buf[slot, j, pl.ds(first, depth // 2), :],
                        (((1,), (1,)), ((), ())),
                        preferred_element_type=F32,
                    )
                    gain_part = gains[:, j * depth + first : j * depth + first + depth // 2]
                    out_buf[slot, :, part] = (
                        back * gain_part - tok_buf[slot, :, part].astype(F32) * less_ref[...]
                    ).astype(BF16)
            for copy in stores(step):
                copy.start()
        for step in range(max(steps - 2, 0), steps):
            for copy in stores(step):
                copy.wait()

    in_specs = [SCALARS, SPACE, LOCAL, LOCAL, LOCAL] + [SPACE] * len(arrays)
    args = [order, tokens, gain, scaled_cot, less, *arrays]
    aliases = {}
    if aliased:
        in_specs.append(SPACE)
        args.append(result)
        aliases = {len(args) - 1: 0}
    return pl.pallas_call(
        body,
        out_shape=jax.ShapeDtypeStruct((rows, width), BF16),
        in_specs=in_specs,
        out_specs=SPACE,
        input_output_aliases=aliases,
        scratch_shapes=[
            pltpu.VMEM((2, rows, 2 * depth), BF16),
            pltpu.VMEM((2, 2, depth, outs), BF16),
            pltpu.VMEM((2, rows, 2 * depth), BF16),
            pltpu.SemaphoreType.DMA((2, 2)),
            pltpu.SemaphoreType.DMA((2, 2)),
            pltpu.SemaphoreType.DMA((2, 2)),
        ],
        compiler_params=params(),
        cost_estimate=COST,
    )(*args)


def sums(groups, half, targets=()):
    terms = [term for halves_of in groups for items in halves_of for term in items]
    width = terms[0][0].shape[1]
    step = half // 2

    def view(array):
        return array.reshape(-1, half, width)

    def body(*refs):
        outs = refs[len(terms) :]
        k = 0
        for out, halves_of in zip(outs, groups):
            for part, items in enumerate(halves_of):
                total = refs[k][0].astype(F32)
                for j in range(1, len(items)):
                    total = total + refs[k + j][0].astype(F32)
                k += len(items)
                out[part] = total.astype(BF16)

    def term_spec(part):
        return pl.BlockSpec((1, step, width), lambda j: (part, j, 0))

    shapes = [
        (view(terms[targets[o]][0]).shape[0] if targets else len(halves_of), half, width)
        for o, halves_of in enumerate(groups)
    ]
    results = pl.pallas_call(
        body,
        out_shape=tuple(jax.ShapeDtypeStruct(shape, BF16) for shape in shapes),
        grid=(2,),
        in_specs=[term_spec(part) for _, part in terms],
        out_specs=tuple(
            pl.BlockSpec((len(halves_of), step, width), lambda j: (0, j, 0))
            for halves_of in groups
        ),
        input_output_aliases={term: o for o, term in enumerate(targets)},
        compiler_params=params(),
        cost_estimate=COST,
    )(*[view(array) for array, _ in terms])
    return [result.reshape(-1, width) for result in results]


def rearrange(sources, moves, shapes):
    def body(*refs):
        ins, outs = refs[: len(sources)], refs[len(sources) : len(sources) + len(shapes)]
        buf, in_sem, out_sem = refs[-3:]

        def load(k):
            i, start, n, _ = moves[k]
            return pltpu.make_async_copy(
                ins[i].at[pl.ds(start, n)], buf.at[k, pl.ds(0, n)], in_sem.at[k]
            )

        def stores(k):
            n, places = moves[k][2:]
            copies = []
            for j, (o, lead, first) in enumerate(places):
                target = outs[o] if lead is None else outs[o].at[lead]
                copies.append(
                    pltpu.make_async_copy(
                        buf.at[k, pl.ds(0, n)], target.at[pl.ds(first, n)], out_sem.at[k, j]
                    )
                )
            return copies

        for k in range(len(moves)):
            load(k).start()
        for k in range(len(moves)):
            load(k).wait()
            for copy in stores(k):
                copy.start()
        for k in range(len(moves)):
            for copy in stores(k):
                copy.wait()

    rows = max(n for _, _, n, _ in moves)
    return pl.pallas_call(
        body,
        out_shape=tuple(jax.ShapeDtypeStruct(shape, BF16) for shape in shapes),
        in_specs=[SPACE] * len(sources),
        out_specs=(SPACE,) * len(shapes),
        scratch_shapes=[
            pltpu.VMEM((len(moves), rows, sources[0].shape[1]), BF16),
            pltpu.SemaphoreType.DMA((len(moves),)),
            pltpu.SemaphoreType.DMA((len(moves), 3)),
        ],
        compiler_params=params(),
        cost_estimate=COST,
    )(*sources)


def after(values, *earlier):
    return lax.optimization_barrier((values, earlier))[0]


def per_device(
    tokens, gain, value_weight, cotangent, codes, scales, local_frag, momentum, global_frag
):
    groups = NX * NZ * NC
    gain_row = gain[None]
    own = value_weight[0]
    depth = own.shape[0]
    half = depth // 2
    early = halves((ZX2, ZZ, ZXP, ZXM))
    late = [(X2, 1), (XP, 0), (X2, 0), (XM, 1), (XP, 1), (XM, 0), (OWN, 0), (OWN, 1)]
    far_three = FAR[:-1]
    table = order_table(
        (
            (1, early + late),
            (0, early),
            (0, late),
            (0, NEAR),
            (1, NEAR),
            (0, far_three),
            (1, far_three),
            (0, FAR[-1:]),
            (1, FAR[-1:]),
        )
    )
    pair_count = len(early) // 2
    at_early, at_late, at_near = 4 * pair_count, 6 * pair_count, 8 * pair_count
    at_near_swap, at_far = at_near + len(NEAR), at_near + 2 * len(NEAR)
    at_last = at_far + 2 * len(far_three)

    xm = move(own, dx=1)
    xp = move(own, dx=-1)
    zz = move(own, dz=1)

    codes, local_frag = codes[0], local_frag[0]
    rows, frag_width = codes.shape
    blocks = scales.shape[2]
    delta = (
        (
            codes.astype(F32).reshape(rows, blocks, frag_width // blocks)
            * scales[0].astype(F32)[..., None]
        )
        .reshape(rows, frag_width)
        .astype(BF16)
    )
    me = lax.axis_index("rep")
    low, high, h = (me // NH) % 2, me // NH // 2, me % NH
    wide = frag_width // NY
    piece = wide // NH

    def cut(value, k, size):
        return lax.dynamic_slice_in_dim(value, k * size, size, axis=1)

    def low_half(bit):
        return jnp.concatenate(
            [cut(delta[:, : 2 * wide], bit, wide), cut(delta[:, 2 * wide :], bit, wide)], axis=1
        )

    kept, leaving = low_half(low), low_half(1 - low)
    got = swap_rep(leaving, y_bit=1)
    tokens_after, cot_after = after((tokens, cotangent), kept, leaving)
    rinv, scaled_cot = statistics(tokens_after, cot_after)
    sent_terms, sent_late = weight_terms(
        tokens, gain_row, scaled_cot, (table, 0, 2 * pair_count), groups
    )

    kept, got = after((kept, got), sent_terms)
    total = kept.astype(F32) + got.astype(F32)
    kept, leaving = cut(total, high, wide), cut(total, 1 - high, wide).astype(BF16)
    got = swap_rep(leaving, y_bit=2)

    xm, xp, zz = after((xm, xp, zz), sent_terms, kept, leaving)
    near_shape = (len(NEAR), depth, own.shape[1])
    m_p, m_m, near = rearrange(
        (own, xp, xm, zz),
        (
            (2, 0, half, [(0, None, 0), (2, 2, 0)]),
            (1, half, half, [(1, None, 0), (2, 1, half)]),
            (3, 0, half, [(0, None, half), (1, None, half), (2, 3, 0)]),
            (3, half, half, [(0, None, depth), (1, None, depth), (2, 3, half)]),
            (2, half, half, [(2, 2, half)]),
            (1, 0, half, [(2, 1, 0)]),
            (0, 0, half, [(2, 0, 0)]),
            (0, half, half, [(2, 0, half)]),
        ),
        ((half + depth, near_shape[2]), (half + depth, near_shape[2]), near_shape),
    )
    r_p = move(m_p, dx=1)
    r_m = move(m_m, dx=-1)
    got_terms = move(after(sent_terms, m_p), dc=1)
    near_other = move(near, dc=1)
    near_list = [(near, k) for k in range(len(NEAR))]
    near_other_list = [(near_other, k) for k in range(len(NEAR))]

    partial = forward(
        tokens, gain_row, (table, at_near), near_list, None
    )
    p_zx2, p_zz = weight_terms(
        tokens, gain_row, scaled_cot, (after(table, partial), at_early, 2), groups,
        got_terms, 0,
    )
    c_x2 = move(p_zx2, dz=1)
    p_zxp, p_zxm = weight_terms(
        tokens, gain_row, scaled_cot, (after(table, p_zx2), at_early + 4, 2), groups,
        got_terms, 2,
    )
    kept, got = after((kept, got), p_zxp)
    total = kept + got.astype(F32)
    kept, leaving = cut(total, h, piece), cut(total, 1 - h, piece).astype(BF16)
    partial = forward(
        tokens, gain_row, (after(table, kept, leaving), at_near_swap), near_other_list, partial
    )
    r_p, r_m, c_x2 = after((r_p, r_m, c_x2), partial)
    x2, far = rearrange(
        (r_p, r_m),
        (
            (0, 0, half, [(0, None, 0), (1, 0, 0)]),
            (1, 0, half, [(0, None, half), (1, 0, half)]),
            (1, half, depth, [(1, 1, 0)]),
            (0, half, depth, [(1, 2, 0)]),
        ),
        ((depth, own.shape[1]), (len(FAR) - 1, depth, own.shape[1])),
    )
    zx2 = move(x2, dz=1)
    got = swap_rep(after(leaving, x2), h_bit=1)
    far_other = move(far, dc=1)
    s_zxp, s_zxm = after((p_zxp, p_zxm), x2)
    a_p = move(s_zxp, dx=1)
    a_m = move(s_zxm, dx=-1)
    p_m1, p_m2, p_ends, p_own = weight_terms(
        tokens,
        gain_row,
        scaled_cot,
        (after(table, x2), at_late, pair_count),
        groups,
        move(after(sent_late, x2), dc=1),
        0,
    )

    c_x2, p_m1, p_m2 = after((c_x2, p_m1, p_m2), p_own)
    m1, m2 = sums(
        ([[(p_m1, 0), (c_x2, 1)]], [[(p_m2, 0), (c_x2, 0)]]),
        half,
        (0, 2),
    )
    d1 = move(m1, dx=1)
    d2 = move(m2, dx=-1)
    far_list = [(far, k) for k in range(len(far_three))]
    far_other_list = [(far_other, k) for k in range(len(far_three))]
    partial = forward(
        tokens, gain_row, (after(table, m1, m2), at_far), far_list + far_other_list, partial
    )
    a_p, a_m, p_zz, zx2, kept, got = after((a_p, a_m, p_zz, zx2, kept, got), partial)
    average = (kept + got.astype(F32)) / (NY * NH)
    new_momentum = 0.9 * momentum + average
    new_global = global_frag - 0.7 * (average + 0.9 * new_momentum)
    sent = new_global.astype(BF16)

    zx2_other = move(zx2, dc=1)
    (e_zz,) = sums(
        ([[(p_zz, 0), (a_p, 0), (a_m, 0)], [(p_zz, 1), (a_p, 1), (a_m, 1)]],),
        half,
    )
    f_z = move(e_zz, dz=1)
    got = swap_rep(after(sent, e_zz), h_bit=1)
    last_list = [(zx2, None), (zx2_other, None)]
    values, less = forward(
        tokens, gain_row, (after(table, e_zz), at_last), last_list, partial, (rinv, scaled_cot)
    )
    sent, got = after((sent, got), values)
    pair = jnp.where(
        h == 0, jnp.concatenate([sent, got], axis=1), jnp.concatenate([got, sent], axis=1)
    )
    got = swap_rep(pair, y_bit=2)

    def back(order, sources, result):
        return backward(tokens, gain_row, scaled_cot, less, order, sources, result)

    token_gradient = back(
        (after(table, pair), at_near), near_list + near_other_list, None
    )
    d1, d2, p_ends = after((d1, d2, p_ends), token_gradient)
    f1, f2 = sums(
        ([[(p_ends, 0), (d1, 0)]], [[(p_ends, 1), (d2, 0)]]), half
    )
    f_p = move(f1, dx=1)
    f_m = move(f2, dx=-1)
    pair, got = after((pair, got), f1, f2)
    quad = jnp.where(
        high == 0, jnp.concatenate([pair, got], axis=1), jnp.concatenate([got, pair], axis=1)
    )
    got = swap_rep(quad, y_bit=1)
    token_gradient = back(
        (after(table, quad), at_far), far_list + far_other_list + last_list, token_gradient
    )
    quad, got = after((quad, got), token_gradient)
    even, odd = jnp.where(low == 0, quad, got), jnp.where(low == 0, got, quad)
    full = jnp.concatenate(
        [even[:, :wide], odd[:, :wide], even[:, wide:], odd[:, wide:]], axis=1
    )
    merged = (0.5 * local_frag.astype(F32) + 0.5 * full.astype(F32)).astype(BF16)
    f_z, f_p, f_m, p_own = after((f_z, f_p, f_m, p_own), merged)
    (weight_grad,) = sums(
        (
            [
                [(p_own, 0), (d1, 1), (f_z, 0), (f_m, 0)],
                [(p_own, 1), (d2, 1), (f_z, 1), (f_p, 0)],
            ],
        ),
        half,
    )
    return (
        values,
        token_gradient,
        weight_grad[None],
        merged[None],
        new_momentum,
        new_global,
    )


def solution(mesh):
    return jax.shard_map(
        per_device,
        mesh=mesh,
        in_specs=(
            P(("rep", "fsdp"), None),
            P(),
            P("rep", "fsdp", None),
            P(("rep", "fsdp"), None),
            P("rep", "fsdp", None),
            P("rep", "fsdp", None),
            P("rep", "fsdp", None),
            P("fsdp", "rep"),
            P("fsdp", "rep"),
        ),
        out_specs=(
            P(("rep", "fsdp"), None),
            P(("rep", "fsdp"), None),
            P("rep", "fsdp", None),
            P("rep", "fsdp", None),
            P("fsdp", "rep"),
            P("fsdp", "rep"),
        ),
        check_vma=False,
    )
```

```python
import jax
import jax.numpy as jnp
from jax import lax
from jax.experimental import pallas as pl
from jax.experimental.pallas import tpu as pltpu
from jax.sharding import PartitionSpec as P

F32 = jnp.float32
BF16 = jnp.bfloat16
NX, NZ, NC, NY, NH = 4, 2, 2, 4, 2
OWN, XP, XM, ZZ = (0, 0), (1, 0), (3, 0), (0, 1)
X2, ZXP, ZXM, ZX2 = (2, 0), (1, 1), (3, 1), (2, 1)
NEAR = (OWN, XP, XM, ZZ)
FAR = (X2, ZXP, ZXM, ZX2)
VMEM = 62 * 2**20


def fsdp_index(x, z, c):
    return ((x % NX) * NZ + z % NZ) * NC + c % NC


def move(value, dx=0, dz=0, dc=0):
    pairs = [
        (fsdp_index(x, z, c), fsdp_index(x + dx, z + dz, c + dc))
        for x in range(NX)
        for z in range(NZ)
        for c in range(NC)
    ]
    return lax.ppermute(value, "fsdp", pairs)


def swap_rep(value, y_bit=0, h_bit=0):
    pairs = [(y * NH + h, (y ^ y_bit) * NH + (h ^ h_bit)) for y in range(NY) for h in range(NH)]
    return lax.ppermute(value, "rep", pairs)


def halves(places):
    return [(place, part) for place in places for part in (0, 1)]


def order_table(lists):
    me = lax.axis_index("fsdp")
    x, z, c = me // (NZ * NC), (me // NC) % NZ, me % NC
    table = []
    for dc, items in lists:
        for item in items:
            (dx, dz), part = item if isinstance(item[0], tuple) else (item, None)
            index = fsdp_index(x + dx, z + dz, c + dc)
            table.append(index if part is None else index * 2 + part)
    return jnp.stack(table).astype(jnp.int32)


def params():
    return pltpu.CompilerParams(vmem_limit_bytes=VMEM)


SPACE = pl.BlockSpec(memory_space=pltpu.HBM)
LOCAL = pl.BlockSpec(memory_space=pltpu.VMEM)
SCALARS = pl.BlockSpec(memory_space=pltpu.SMEM)
COST = pl.CostEstimate(flops=1, bytes_accessed=1, transcendentals=0)


def statistics(tokens, cotangent):
    rows, width = tokens.shape
    outs = cotangent.shape[1]
    parts = 8
    step = rows // parts

    def body(tok_ref, cot_ref, rinv_ref, scaled_ref, buf, sem):
        def load(k):
            return pltpu.make_async_copy(
                tok_ref.at[pl.ds(k * step, step)], buf.at[k], sem.at[k]
            )

        for k in range(parts):
            load(k).start()
        lanes = 512
        for k in range(parts):
            load(k).wait()
            total = jnp.zeros((step, lanes), F32)
            for first in range(0, width, lanes):
                value = buf[k, :, first : first + lanes].astype(F32)
                total = total + value * value
            mean = jnp.sum(total, axis=-1, keepdims=True) / width
            rinv = 1.0 / jnp.sqrt(mean + 1e-05)
            part = pl.ds(k * step, step)
            rinv_ref[part, :] = rinv
            scaled_ref[part, :] = (cot_ref[part, :].astype(F32) * rinv).astype(BF16)

    return pl.pallas_call(
        body,
        out_shape=(
            jax.ShapeDtypeStruct((rows, 1), F32),
            jax.ShapeDtypeStruct((rows, outs), BF16),
        ),
        in_specs=[SPACE, LOCAL],
        out_specs=(LOCAL, LOCAL),
        scratch_shapes=[
            pltpu.VMEM((parts, step, width), BF16),
            pltpu.SemaphoreType.DMA((parts,)),
        ],
        compiler_params=params(),
        cost_estimate=COST,
    )(tokens, cotangent)


def unit_columns(order_ref, k, unit):
    return pl.ds(pl.multiple_of(order_ref[k] * unit, unit), unit)


def token_copies(order_ref, base, tok_ref, buf, sem, step, unit, per):
    slot = step % 2
    return [
        pltpu.make_async_copy(
            tok_ref.at[:, unit_columns(order_ref, base + step * per + u, unit)],
            buf.at[slot, :, pl.ds(u * unit, unit)],
            sem.at[slot, u],
        )
        for u in range(per)
    ]


def unit_gain(order_ref, base, gain_ref, step, unit, per):
    return jnp.concatenate(
        [gain_ref[:, unit_columns(order_ref, base + step * per + u, unit)] for u in range(per)],
        axis=1,
    )


def weight_terms(tokens, gain, scaled_cot, order, groups, other=None, first=0):
    rows, width = tokens.shape
    outs = scaled_cot.shape[1]
    unit = width // (NX * NZ * NC * 2)
    order, base, count = order
    depth = 2 * unit
    steps = count // 2

    def body(order_ref, tok_ref, gain_ref, cot_ref, *rest):
        if other is None:
            *out_refs, tok_buf, out_buf, tok_sem, out_sem = rest
            targets = [ref.at[k] for ref in out_refs for k in range(count // 2)]
        else:
            other_ref, targets = rest[0], rest[1 : 1 + count]
            tok_buf, out_buf, tok_sem, out_sem, other_buf, other_sem = rest[1 + count :]

        def loads(step):
            copies = token_copies(order_ref, base, tok_ref, tok_buf, tok_sem, step, unit, 4)
            if other is not None:
                copies += [
                    pltpu.make_async_copy(
                        other_ref.at[first + 2 * step + j],
                        other_buf.at[step % 2, j],
                        other_sem.at[step % 2, j],
                    )
                    for j in range(2)
                ]
            return copies

        def stores(step):
            return [
                pltpu.make_async_copy(
                    out_buf.at[step % 2, j], targets[2 * step + j], out_sem.at[step % 2, j]
                )
                for j in range(2)
            ]

        for copy in loads(0):
            copy.start()
        for step in range(steps):
            slot = step % 2
            if step + 1 < steps:
                for copy in loads(step + 1):
                    copy.start()
            for copy in loads(step):
                copy.wait()
            gains = unit_gain(order_ref, base, gain_ref, step, unit, 4)
            if step >= 2:
                for copy in stores(step - 2):
                    copy.wait()
            for j in range(2):
                for row in range(0, depth, unit):
                    start = j * depth + row
                    left = (
                        tok_buf[slot, :, pl.ds(start, unit)].astype(F32)
                        * gains[:, start : start + unit]
                    ).astype(BF16)
                    term = lax.dot_general(
                        left, cot_ref[...], (((0,), (0,)), ((), ())), preferred_element_type=F32
                    ) * (1.0 / groups)
                    if other is not None:
                        term = term + other_buf[slot, j, pl.ds(row, unit), :].astype(F32)
                    out_buf[slot, j, pl.ds(row, unit), :] = term.astype(BF16)
            for copy in stores(step):
                copy.start()
        for step in range(max(steps - 2, 0), steps):
            for copy in stores(step):
                copy.wait()

    scratch = [
        pltpu.VMEM((2, rows, 2 * depth), BF16),
        pltpu.VMEM((2, 2, depth, outs), BF16),
        pltpu.SemaphoreType.DMA((2, 4)),
        pltpu.SemaphoreType.DMA((2, 2)),
    ]
    in_specs, args = [SCALARS, SPACE, LOCAL, LOCAL], [order, tokens, gain, scaled_cot]
    if other is None:
        out_shape = (jax.ShapeDtypeStruct((count // 2, depth, outs), BF16),) * 2
        out_specs = (SPACE,) * 2
    else:
        out_shape = (jax.ShapeDtypeStruct((depth, outs), BF16),) * count
        out_specs = (SPACE,) * count
        in_specs.append(SPACE)
        args.append(other)
        scratch += [pltpu.VMEM((2, 2, depth, outs), BF16), pltpu.SemaphoreType.DMA((2, 2))]
    return pl.pallas_call(
        body,
        out_shape=out_shape,
        in_specs=in_specs,
        out_specs=out_specs,
        scratch_shapes=scratch,
        compiler_params=params(),
        cost_estimate=COST,
    )(*args)


def unique(sources):
    arrays, places = [], []
    for array, where in sources:
        position = next((i for i, known in enumerate(arrays) if known is array), len(arrays))
        if position == len(arrays):
            arrays.append(array)
        places.append((position, where))
    return arrays, places


def weight_copies(refs, places, buf, sem, step):
    copies = []
    for j in range(2):
        position, where = places[2 * step + j]
        source = refs[position] if where is None else refs[position].at[where]
        copies.append(pltpu.make_async_copy(source, buf.at[step % 2, j], sem.at[step % 2, j]))
    return copies


def forward(tokens, gain, order, sources, total, last=None):
    rows, width = tokens.shape
    arrays, places = unique(sources)
    depth, outs = arrays[0].shape[-2:]
    steps, ins = len(places) // 2, len(arrays)
    order, base = order
    rest_in = (0 if total is None else 1) + (0 if last is None else 2)

    def body(order_ref, tok_ref, gain_ref, *rest):
        extra = rest[ins : ins + rest_in]
        results = rest[ins + rest_in : -4]
        tok_buf, w_buf, tok_sem, w_sem = rest[-4:]

        def loads(step):
            return token_copies(
                order_ref, base, tok_ref, tok_buf, tok_sem, step, depth, 2
            ) + weight_copies(rest[:ins], places, w_buf, w_sem, step)

        for copy in loads(0):
            copy.start()
        acc = None if total is None else extra[0][...]
        for step in range(steps):
            if step + 1 < steps:
                for copy in loads(step + 1):
                    copy.start()
            for copy in loads(step):
                copy.wait()
            gains = unit_gain(order_ref, base, gain_ref, step, depth, 2)
            left = (tok_buf[step % 2].astype(F32) * gains).astype(BF16)
            term = jnp.dot(
                left, w_buf[step % 2].reshape(2 * depth, outs), preferred_element_type=F32
            )
            acc = term if acc is None else acc + term
        if last is None:
            results[0][...] = acc
        else:
            rinv = extra[-2][...]
            results[0][...] = (acc * rinv).astype(BF16)
            dots = jnp.sum(acc * extra[-1][...].astype(F32), axis=-1, keepdims=True)
            results[1][...] = dots * rinv * rinv * (1.0 / width)

    if last is None:
        out_shape, out_specs = jax.ShapeDtypeStruct((rows, outs), F32), LOCAL
    else:
        out_shape = (
            jax.ShapeDtypeStruct((rows, outs), BF16),
            jax.ShapeDtypeStruct((rows, 1), F32),
        )
        out_specs = (LOCAL, LOCAL)
    return pl.pallas_call(
        body,
        out_shape=out_shape,
        in_specs=[SCALARS, SPACE, LOCAL] + [SPACE] * ins + [LOCAL] * rest_in,
        out_specs=out_specs,
        scratch_shapes=[
            pltpu.VMEM((2, rows, 2 * depth), BF16),
            pltpu.VMEM((2, 2, depth, outs), BF16),
            pltpu.SemaphoreType.DMA((2, 2)),
            pltpu.SemaphoreType.DMA((2, 2)),
        ],
        compiler_params=params(),
        cost_estimate=COST,
    )(order, tokens, gain, *arrays, *(() if total is None else (total,)), *(last or ()))


def backward(tokens, gain, scaled_cot, less, order, sources, result):
    rows, width = tokens.shape
    arrays, places = unique(sources)
    depth, outs = arrays[0].shape[-2:]
    steps = len(places) // 2
    order, base = order
    aliased = result is not None

    def body(order_ref, tok_ref, gain_ref, cot_ref, less_ref, *rest):
        refs = rest[: len(arrays)]
        out_ref, tok_buf, w_buf, out_buf, tok_sem, w_sem, out_sem = rest[-7:]

        def loads(step):
            return token_copies(
                order_ref, base, tok_ref, tok_buf, tok_sem, step, depth, 2
            ) + weight_copies(refs, places, w_buf, w_sem, step)

        def stores(step):
            return [
                pltpu.make_async_copy(
                    out_buf.at[step % 2, :, pl.ds(u * depth, depth)],
                    out_ref.at[:, unit_columns(order_ref, base + step * 2 + u, depth)],
                    out_sem.at[step % 2, u],
                )
                for u in range(2)
            ]

        for copy in loads(0):
            copy.start()
        for step in range(steps):
            slot = step % 2
            if step + 1 < steps:
                for copy in loads(step + 1):
                    copy.start()
            for copy in loads(step):
                copy.wait()
            gains = unit_gain(order_ref, base, gain_ref, step, depth, 2)
            if step >= 2:
                for copy in stores(step - 2):
                    copy.wait()
            for j in range(2):
                for first in range(0, depth, depth // 2):
                    part = pl.ds(j * depth + first, depth // 2)
                    back = lax.dot_general(
                        cot_ref[...],
                        w_buf[slot, j, pl.ds(first, depth // 2), :],
                        (((1,), (1,)), ((), ())),
                        preferred_element_type=F32,
                    )
                    gain_part = gains[:, j * depth + first : j * depth + first + depth // 2]
                    out_buf[slot, :, part] = (
                        back * gain_part - tok_buf[slot, :, part].astype(F32) * less_ref[...]
                    ).astype(BF16)
            for copy in stores(step):
                copy.start()
        for step in range(max(steps - 2, 0), steps):
            for copy in stores(step):
                copy.wait()

    in_specs = [SCALARS, SPACE, LOCAL, LOCAL, LOCAL] + [SPACE] * len(arrays)
    args = [order, tokens, gain, scaled_cot, less, *arrays]
    aliases = {}
    if aliased:
        in_specs.append(SPACE)
        args.append(result)
        aliases = {len(args) - 1: 0}
    return pl.pallas_call(
        body,
        out_shape=jax.ShapeDtypeStruct((rows, width), BF16),
        in_specs=in_specs,
        out_specs=SPACE,
        input_output_aliases=aliases,
        scratch_shapes=[
            pltpu.VMEM((2, rows, 2 * depth), BF16),
            pltpu.VMEM((2, 2, depth, outs), BF16),
            pltpu.VMEM((2, rows, 2 * depth), BF16),
            pltpu.SemaphoreType.DMA((2, 2)),
            pltpu.SemaphoreType.DMA((2, 2)),
            pltpu.SemaphoreType.DMA((2, 2)),
        ],
        compiler_params=params(),
        cost_estimate=COST,
    )(*args)


def sums(groups, half, targets=()):
    terms = [term for halves_of in groups for items in halves_of for term in items]
    width = terms[0][0].shape[1]
    step = half // 2

    def view(array):
        return array.reshape(-1, half, width)

    def body(*refs):
        outs = refs[len(terms) :]
        k = 0
        for out, halves_of in zip(outs, groups):
            for part, items in enumerate(halves_of):
                total = refs[k][0].astype(F32)
                for j in range(1, len(items)):
                    total = total + refs[k + j][0].astype(F32)
                k += len(items)
                out[part] = total.astype(BF16)

    def term_spec(part):
        return pl.BlockSpec((1, step, width), lambda j: (part, j, 0))

    shapes = [
        (view(terms[targets[o]][0]).shape[0] if targets else len(halves_of), half, width)
        for o, halves_of in enumerate(groups)
    ]
    results = pl.pallas_call(
        body,
        out_shape=tuple(jax.ShapeDtypeStruct(shape, BF16) for shape in shapes),
        grid=(2,),
        in_specs=[term_spec(part) for _, part in terms],
        out_specs=tuple(
            pl.BlockSpec((len(halves_of), step, width), lambda j: (0, j, 0))
            for halves_of in groups
        ),
        input_output_aliases={term: o for o, term in enumerate(targets)},
        compiler_params=params(),
        cost_estimate=COST,
    )(*[view(array) for array, _ in terms])
    return [result.reshape(-1, width) for result in results]


def rearrange(sources, moves, shapes):
    def body(*refs):
        ins, outs = refs[: len(sources)], refs[len(sources) : len(sources) + len(shapes)]
        buf, in_sem, out_sem = refs[-3:]

        def load(k):
            i, start, n, _ = moves[k]
            return pltpu.make_async_copy(
                ins[i].at[pl.ds(start, n)], buf.at[k, pl.ds(0, n)], in_sem.at[k]
            )

        def stores(k):
            n, places = moves[k][2:]
            copies = []
            for j, (o, lead, first) in enumerate(places):
                target = outs[o] if lead is None else outs[o].at[lead]
                copies.append(
                    pltpu.make_async_copy(
                        buf.at[k, pl.ds(0, n)], target.at[pl.ds(first, n)], out_sem.at[k, j]
                    )
                )
            return copies

        for k in range(len(moves)):
            load(k).start()
        for k in range(len(moves)):
            load(k).wait()
            for copy in stores(k):
                copy.start()
        for k in range(len(moves)):
            for copy in stores(k):
                copy.wait()

    rows = max(n for _, _, n, _ in moves)
    return pl.pallas_call(
        body,
        out_shape=tuple(jax.ShapeDtypeStruct(shape, BF16) for shape in shapes),
        in_specs=[SPACE] * len(sources),
        out_specs=(SPACE,) * len(shapes),
        scratch_shapes=[
            pltpu.VMEM((len(moves), rows, sources[0].shape[1]), BF16),
            pltpu.SemaphoreType.DMA((len(moves),)),
            pltpu.SemaphoreType.DMA((len(moves), 3)),
        ],
        compiler_params=params(),
        cost_estimate=COST,
    )(*sources)


def after(values, *earlier):
    return lax.optimization_barrier((values, earlier))[0]


def per_device(
    tokens, gain, value_weight, cotangent, codes, scales, local_frag, momentum, global_frag
):
    groups = NX * NZ * NC
    gain_row = gain[None]
    own = value_weight[0]
    depth = own.shape[0]
    half = depth // 2
    early = halves((ZX2, ZZ, ZXP, ZXM))
    late = [(X2, 1), (XP, 0), (X2, 0), (XM, 1), (XP, 1), (XM, 0), (OWN, 0), (OWN, 1)]
    far_three = FAR[:-1]
    table = order_table(
        (
            (1, early + late),
            (0, early),
            (0, late),
            (0, NEAR),
            (1, NEAR),
            (0, far_three),
            (1, far_three),
            (0, FAR[-1:]),
            (1, FAR[-1:]),
        )
    )
    pair_count = len(early) // 2
    at_early, at_late, at_near = 4 * pair_count, 6 * pair_count, 8 * pair_count
    at_near_swap, at_far = at_near + len(NEAR), at_near + 2 * len(NEAR)
    at_last = at_far + 2 * len(far_three)

    xm = move(own, dx=1)
    xp = move(own, dx=-1)
    zz = move(own, dz=1)

    codes, local_frag = codes[0], local_frag[0]
    rows, frag_width = codes.shape
    blocks = scales.shape[2]
    delta = (
        (
            codes.astype(F32).reshape(rows, blocks, frag_width // blocks)
            * scales[0].astype(F32)[..., None]
        )
        .reshape(rows, frag_width)
        .astype(BF16)
    )
    me = lax.axis_index("rep")
    low, high, h = (me // NH) % 2, me // NH // 2, me % NH
    wide = frag_width // NY
    piece = wide // NH

    def cut(value, k, size):
        return lax.dynamic_slice_in_dim(value, k * size, size, axis=1)

    def low_half(bit):
        return jnp.concatenate(
            [cut(delta[:, : 2 * wide], bit, wide), cut(delta[:, 2 * wide :], bit, wide)], axis=1
        )

    kept, leaving = low_half(low), low_half(1 - low)
    got = swap_rep(leaving, y_bit=1)
    tokens_after, cot_after = after((tokens, cotangent), kept, leaving)
    rinv, scaled_cot = statistics(tokens_after, cot_after)
    sent_terms, sent_late = weight_terms(
        tokens, gain_row, scaled_cot, (table, 0, 2 * pair_count), groups
    )

    kept, got = after((kept, got), sent_terms)
    total = kept.astype(F32) + got.astype(F32)
    kept, leaving = cut(total, high, wide), cut(total, 1 - high, wide).astype(BF16)
    got = swap_rep(leaving, y_bit=2)

    xm, xp, zz = after((xm, xp, zz), sent_terms, kept, leaving)
    near_shape = (len(NEAR), depth, own.shape[1])
    m_p, m_m, near = rearrange(
        (own, xp, xm, zz),
        (
            (2, 0, half, [(0, None, 0), (2, 2, 0)]),
            (1, half, half, [(1, None, 0), (2, 1, half)]),
            (3, 0, half, [(0, None, half), (1, None, half), (2, 3, 0)]),
            (3, half, half, [(0, None, depth), (1, None, depth), (2, 3, half)]),
            (2, half, half, [(2, 2, half)]),
            (1, 0, half, [(2, 1, 0)]),
            (0, 0, half, [(2, 0, 0)]),
            (0, half, half, [(2, 0, half)]),
        ),
        ((half + depth, near_shape[2]), (half + depth, near_shape[2]), near_shape),
    )
    r_p = move(m_p, dx=1)
    r_m = move(m_m, dx=-1)
    got_terms = move(after(sent_terms, m_p), dc=1)
    near_other = move(near, dc=1)
    near_list = [(near, k) for k in range(len(NEAR))]
    near_other_list = [(near_other, k) for k in range(len(NEAR))]

    partial = forward(
        tokens, gain_row, (table, at_near), near_list, None
    )
    p_zx2, p_zz = weight_terms(
        tokens, gain_row, scaled_cot, (after(table, partial), at_early, 2), groups,
        got_terms, 0,
    )
    c_x2 = move(p_zx2, dz=1)
    p_zxp, p_zxm = weight_terms(
        tokens, gain_row, scaled_cot, (after(table, p_zx2), at_early + 4, 2), groups,
        got_terms, 2,
    )
    kept, got = after((kept, got), p_zxp)
    total = kept + got.astype(F32)
    kept, leaving = cut(total, h, piece), cut(total, 1 - h, piece).astype(BF16)
    partial = forward(
        tokens, gain_row, (after(table, kept, leaving), at_near_swap), near_other_list, partial
    )
    r_p, r_m, c_x2 = after((r_p, r_m, c_x2), partial)
    x2, far = rearrange(
        (r_p, r_m),
        (
            (0, 0, half, [(0, None, 0), (1, 0, 0)]),
            (1, 0, half, [(0, None, half), (1, 0, half)]),
            (1, half, depth, [(1, 1, 0)]),
            (0, half, depth, [(1, 2, 0)]),
        ),
        ((depth, own.shape[1]), (len(FAR) - 1, depth, own.shape[1])),
    )
    zx2 = move(x2, dz=1)
    got = swap_rep(after(leaving, x2), h_bit=1)
    far_other = move(far, dc=1)
    s_zxp, s_zxm = after((p_zxp, p_zxm), x2)
    a_p = move(s_zxp, dx=1)
    a_m = move(s_zxm, dx=-1)
    p_m1, p_m2, p_ends, p_own = weight_terms(
        tokens,
        gain_row,
        scaled_cot,
        (after(table, x2), at_late, pair_count),
        groups,
        move(after(sent_late, x2), dc=1),
        0,
    )

    c_x2, p_m1, p_m2 = after((c_x2, p_m1, p_m2), p_own)
    m1, m2 = sums(
        ([[(p_m1, 0), (c_x2, 1)]], [[(p_m2, 0), (c_x2, 0)]]),
        half,
        (0, 2),
    )
    d1 = move(m1, dx=1)
    d2 = move(m2, dx=-1)
    far_list = [(far, k) for k in range(len(far_three))]
    far_other_list = [(far_other, k) for k in range(len(far_three))]
    partial = forward(
        tokens, gain_row, (after(table, m1, m2), at_far), far_list + far_other_list, partial
    )
    a_p, a_m, p_zz = after((a_p, a_m, p_zz), partial)
    (e_zz,) = sums(
        ([[(p_zz, 0), (a_p, 0), (a_m, 0)], [(p_zz, 1), (a_p, 1), (a_m, 1)]],),
        half,
    )
    zx2, kept, got = after((zx2, kept, got), e_zz)
    average = (kept + got.astype(F32)) / (NY * NH)
    new_momentum = 0.9 * momentum + average
    new_global = global_frag - 0.7 * (average + 0.9 * new_momentum)
    sent = new_global.astype(BF16)

    zx2_other = move(zx2, dc=1)
    f_z = move(e_zz, dz=1)
    got = swap_rep(after(sent, e_zz), h_bit=1)
    last_list = [(zx2, None), (zx2_other, None)]
    values, less = forward(
        tokens, gain_row, (after(table, e_zz), at_last), last_list, partial, (rinv, scaled_cot)
    )
    sent, got = after((sent, got), values)
    pair = jnp.where(
        h == 0, jnp.concatenate([sent, got], axis=1), jnp.concatenate([got, sent], axis=1)
    )
    got = swap_rep(pair, y_bit=2)

    def back(order, sources, result):
        return backward(tokens, gain_row, scaled_cot, less, order, sources, result)

    token_gradient = back(
        (after(table, pair), at_near), near_list + near_other_list, None
    )
    d1, d2, p_ends = after((d1, d2, p_ends), token_gradient)
    f1, f2 = sums(
        ([[(p_ends, 0), (d1, 0)]], [[(p_ends, 1), (d2, 0)]]), half
    )
    f_p = move(f1, dx=1)
    f_m = move(f2, dx=-1)
    pair, got = after((pair, got), f1, f2)
    quad = jnp.where(
        high == 0, jnp.concatenate([pair, got], axis=1), jnp.concatenate([got, pair], axis=1)
    )
    got = swap_rep(quad, y_bit=1)
    token_gradient = back(
        (after(table, quad), at_far), far_list + far_other_list + last_list, token_gradient
    )
    quad, got = after((quad, got), token_gradient)
    even, odd = jnp.where(low == 0, quad, got), jnp.where(low == 0, got, quad)
    full = jnp.concatenate(
        [even[:, :wide], odd[:, :wide], even[:, wide:], odd[:, wide:]], axis=1
    )
    merged = (0.5 * local_frag.astype(F32) + 0.5 * full.astype(F32)).astype(BF16)
    f_z, f_p, f_m, p_own = after((f_z, f_p, f_m, p_own), merged)
    (weight_grad,) = sums(
        (
            [
                [(p_own, 0), (d1, 1), (f_z, 0), (f_m, 0)],
                [(p_own, 1), (d2, 1), (f_z, 1), (f_p, 0)],
            ],
        ),
        half,
    )
    return (
        values,
        token_gradient,
        weight_grad[None],
        merged[None],
        new_momentum,
        new_global,
    )


def solution(mesh):
    return jax.shard_map(
        per_device,
        mesh=mesh,
        in_specs=(
            P(("rep", "fsdp"), None),
            P(),
            P("rep", "fsdp", None),
            P(("rep", "fsdp"), None),
            P("rep", "fsdp", None),
            P("rep", "fsdp", None),
            P("rep", "fsdp", None),
            P("fsdp", "rep"),
            P("fsdp", "rep"),
        ),
        out_specs=(
            P(("rep", "fsdp"), None),
            P(("rep", "fsdp"), None),
            P("rep", "fsdp", None),
            P("rep", "fsdp", None),
            P("fsdp", "rep"),
            P("fsdp", "rep"),
        ),
        check_vma=False,
    )
```
